32 devices in a mesh: shard: 4 (over x, core), ctx: 4 (over z), tensor: 2 (over y).
Axes of the slice: x: 2, y: 2, z: 4, core: 2. Of those that a mesh axis runs over, the one named last changes fastest.
Arguments:
- block_in: bfloat16 [8, 2048, 2048], P('shard', 'ctx'), may hold values from -6 to 6
- layer_norm_params: bfloat16 [2, 2048], P(None, ('shard', 'ctx')), may hold values from -0.91 to 2.47, as said below
- w_qkv: bfloat16 [2048, 3, 2048], P(('shard', 'ctx'), None, 'tensor'), may hold values from -0.125 to 0.125
- b_qkv: bfloat16 [3, 2048], P(None, 'tensor'), may hold values from -4 to 4
- w_out: bfloat16 [2048, 2048], P('tensor', ('shard', 'ctx')), may hold values from -2 to 2
- w_fc1: bfloat16 [2048, 8192], P(('shard', 'ctx'), 'tensor'), may hold values from -0.125 to 0.125
- b_fc1: bfloat16 [8192], P('tensor'), may hold values from -6 to 6
- w_fc2: bfloat16 [8192, 2048], P('tensor', ('shard', 'ctx')), may hold values from -0.0625 to 0.0625
- out_biases: bfloat16 [2, 2048], P(None, ('shard', 'ctx')), may hold values from -4 to 4
- cotangent: bfloat16 [8, 2048, 2048], P('shard', 'ctx'), may hold values from -6 to 6
Outputs:
- output: bfloat16 [8, 2048, 2048], P('shard', 'ctx')
- grad_block_in: bfloat16 [8, 2048, 2048], P('shard', 'ctx')
- grad_norm_params: float32 [2, 2048], P(None, ('shard', 'ctx'))
- grad_w_qkv: float32 [2048, 3, 2048], P(('shard', 'ctx'), None, 'tensor')
- grad_b_qkv: float32 [3, 2048], P(None, 'tensor')
- grad_w_out: float32 [2048, 2048], P('tensor', ('shard', 'ctx'))
- grad_w_fc1: float32 [2048, 8192], P(('shard', 'ctx'), 'tensor')
- grad_b_fc1: float32 [8192], P('tensor')
- grad_w_fc2: float32 [8192, 2048], P('tensor', ('shard', 'ctx'))
- grad_out_biases: float32 [2, 2048], P(None, ('shard', 'ctx'))
The draws below stay inside these ranges and needn't reach their ends.
Inputs may be any that keep to these rules, and one draw needn't show every extreme that they name: `layer_norm_params`: row 0 is positive.
All inputs are finite; a program needn't handle non-finite values.
Results may differ from the reference program's by a relative error of at most 0.011.
Values may be sent and summed in bfloat16 or wider, within the bound.
A program may use at most 384 MiB of HBM per device.

```python
import math
import jax
import jax.numpy as jnp
from jax import lax

D = 2048
HEADS = 32
HEAD_DIM = 64
ROT = 32
FF = 8192
LEN = 2048
BATCH = 8


def draw_layer_norm_params(key, part):
    key = jax.random.fold_in(key, 11)
    leading, trailing = jax.random.split(key)
    gain_vector = jnp.exp(0.3 * jnp.clip(jax.random.normal(leading, (D,), jnp.float32), -3.0, 3.0))
    shifts = 0.3 * jnp.clip(jax.random.normal(trailing, (D,), jnp.float32), -3.0, 3.0)
    return jnp.stack([gain_vector, shifts]).astype(jnp.bfloat16)


def block_levels(rng, extent, cuts, low, high):
    gain, own = 1.0, jax.random.fold_in(rng, 6)
    for axis_at, blocks in cuts:
        draws = jnp.exp(jax.random.uniform(jax.random.fold_in(own, axis_at), (blocks,), jnp.float32, low / len(cuts), high / len(cuts)))
        gain = gain * jnp.repeat(draws, extent[axis_at] // blocks).reshape([-1 if axis == axis_at else 1 for axis in range(len(extent))])
    return gain


def normal_values(rng, shape, deviation, bound, cuts=(), held_as=jnp.bfloat16):
    level = block_levels(rng, shape, cuts, -0.22, 0.18) if cuts else 1.0
    drawn = jax.random.normal(rng, shape, jnp.float32) * deviation * level
    return jnp.minimum(jnp.maximum(drawn, -bound), bound).astype(held_as)


def setup_inputs(seed: int = 0) -> dict:
    keys = jax.random.split(jax.random.key(seed), 11)
    return {
        "block_in": normal_values(keys[0], (BATCH, LEN, D), 1.0, 6.0, ((0, 4), (1, 4))),
        "layer_norm_params": draw_layer_norm_params(jax.random.fold_in(keys[10], 71), 0),
        "w_qkv": normal_values(keys[2], (D, 3, D), D ** -0.5, 0.125, ((0, 16), (2, 2))),
        "b_qkv": normal_values(keys[3], (3, D), 0.3, 4.0, ((1, 2),)),
        "w_out": normal_values(keys[4], (D, D), (max(D // 256, 2)) ** -0.5, 2.0, ((0, 2), (1, 16))),
        "w_fc1": normal_values(keys[5], (D, FF), D ** -0.5, 0.125, ((0, 16), (1, 2))),
        "b_fc1": normal_values(keys[6], (FF,), 0.5, 6.0, ((0, 2),)),
        "w_fc2": normal_values(keys[7], (FF, D), FF ** -0.5, 0.0625, ((0, 2), (1, 16))),
        "out_biases": normal_values(keys[8], (2, D), 0.3, 4.0, ((1, 16),)),
        "cotangent": normal_values(keys[9], (BATCH, LEN, D), 1.0, 6.0, ((0, 4), (1, 4))),
    }


NORM_EPSILON = 1e-05
MASKED = -1000000000.0
HIGHEST = lax.Precision.HIGHEST

@jax.custom_vjp
def reduced_precision(v):
    return lax.optimization_barrier(v.astype(jnp.bfloat16)).astype(jnp.float32)

@jax.custom_vjp
def low_back(v):
    return v

def low_keep(v):
    return (reduced_precision(v), None)

def low_pass(kept, grad):
    return (grad,)

def back_keep(v):
    return (v, None)

def back_low(kept, grad):
    return (reduced_precision(grad),)
reduced_precision.defvjp(low_keep, low_pass)
low_back.defvjp(back_keep, back_low)

def tables(length):
    halfway = ROT // 2
    frequency = 10000.0 ** (-(jnp.arange(halfway).astype(jnp.float32) * 2.0 / ROT))
    angles = jnp.arange(length).astype(jnp.float32)[:, None] * frequency[None, :]
    return (jnp.cos(angles), jnp.sin(angles))

def rotate(field, cos_rows, sin_rows):
    halfway = cos_rows.shape[-1]
    leading = field[..., :halfway]
    trailing = field[..., halfway:2 * halfway]
    remainder = field[..., 2 * halfway:]
    cos_bc = cos_rows[:, None, :]
    sin_bc = sin_rows[:, None, :]
    return jnp.concatenate([leading * cos_bc - trailing * sin_bc, trailing * cos_bc + leading * sin_bc, remainder], axis=-1)

def attend(triple):
    queries, keys_rot, values = triple
    scores = low_back(jnp.dot(queries, keys_rot.T, precision=HIGHEST, preferred_element_type=jnp.float32) * HEAD_DIM ** (-0.5))
    positions = jnp.arange(LEN)
    scores = jnp.where(positions[:, None] >= positions[None, :], scores, MASKED)
    weights = reduced_precision(jax.nn.softmax(scores, axis=-1))
    return jnp.dot(weights, values, precision=HIGHEST, preferred_element_type=jnp.float32)

def layer(tokens, layer_norm_params, w_qkv, b_qkv, w_out, w_fc1, b_fc1, w_fc2, out_biases):
    grouped = tokens.shape[0]
    average = lax.optimization_barrier(jnp.mean(tokens, axis=-1, keepdims=True))
    mean_removed = tokens - average
    row_variance = lax.optimization_barrier(jnp.mean(mean_removed * mean_removed, axis=-1, keepdims=True))
    standardized_input = mean_removed * lax.rsqrt(row_variance + NORM_EPSILON)
    normalized_rows = reduced_precision(standardized_input * layer_norm_params[0] + layer_norm_params[1])
    projected = low_back(jnp.einsum('gld,dce->glce', normalized_rows, w_qkv, precision=HIGHEST) + b_qkv)
    split_heads = projected.reshape(grouped, LEN, 3, HEADS, HEAD_DIM)
    cos_rows, sin_rows = tables(LEN)
    queries = reduced_precision(rotate(split_heads[:, :, 0], cos_rows, sin_rows))
    keys_rot = reduced_precision(rotate(split_heads[:, :, 1], cos_rows, sin_rows))
    values = reduced_precision(split_heads[:, :, 2])

    def flatten(field):
        return field.transpose(0, 2, 1, 3).reshape(grouped * HEADS, LEN, HEAD_DIM)
    mixed = lax.map(jax.checkpoint(attend), (flatten(queries), flatten(keys_rot), flatten(values)))
    mixed = mixed.reshape(grouped, HEADS, LEN, HEAD_DIM).transpose(0, 2, 1, 3).reshape(grouped, LEN, D)
    mixed = low_back(reduced_precision(mixed))
    attention = jnp.einsum('gle,ed->gld', mixed, w_out, precision=HIGHEST)
    hidden_pre = low_back(jnp.einsum('gld,df->glf', normalized_rows, w_fc1, precision=HIGHEST) + b_fc1)
    hidden = reduced_precision(jax.nn.gelu(hidden_pre, approximate=True))
    feed = jnp.einsum('glf,fd->gld', hidden, w_fc2, precision=HIGHEST)
    return tokens + attention + feed + out_biases[0] + out_biases[1]

def reference(block_in, layer_norm_params, w_qkv, b_qkv, w_out, w_fc1, b_fc1, w_fc2, out_biases, cotangent):
    params = tuple((weight.astype(jnp.float32) for weight in (layer_norm_params, w_qkv, b_qkv, w_out, w_fc1, b_fc1, w_fc2, out_biases)))
    grouped = math.gcd(BATCH, max(1, 4096 // LEN))
    inputs = block_in.astype(jnp.float32).reshape(BATCH // grouped, grouped, LEN, D)
    cotangents = cotangent.astype(jnp.float32).reshape(BATCH // grouped, grouped, LEN, D)

    def advance(totals, sample):
        tokens, incoming = sample
        result, pullback = jax.vjp(layer, tokens, *params)
        gradients = pullback(incoming)
        totals = tuple((total + gradient for total, gradient in zip(totals, gradients[1:])))
        return (totals, (result, gradients[0]))
    initial = tuple((jnp.zeros_like(weight) for weight in params))
    totals, (results, grad_inputs) = lax.scan(advance, initial, (inputs, cotangents))
    output = results.reshape(BATCH, LEN, D).astype(jnp.bfloat16)
    grad_block_in = grad_inputs.reshape(BATCH, LEN, D).astype(jnp.bfloat16)
    return (output, grad_block_in, totals[0], totals[1], totals[2], totals[3], totals[4], totals[5], totals[6], totals[7])
```

```python
from functools import partial

import jax
import jax.numpy as jnp
from jax import lax
from jax.experimental import pallas as pl
from jax.experimental.pallas import tpu as pltpu
from jax.sharding import PartitionSpec as P

HEAD_DIM = 64
ROT = 32
NORM_EPSILON = 1e-05
MASKED = -1000000000.0
LANES = 128
F32 = jnp.float32
BF16 = jnp.bfloat16
VMEM_LIMIT = 60 * 1024 * 1024


def params(**kw):
    return pltpu.CompilerParams(vmem_limit_bytes=VMEM_LIMIT, **kw)


def rotation_tables(length):
    half = ROT // 2
    frequency = 10000.0 ** (-(jnp.arange(half).astype(F32) * 2.0 / ROT))
    angles = jnp.arange(length).astype(F32)[:, None] * frequency[None, :]
    cos, sin = jnp.cos(angles), jnp.sin(angles)
    zero = jnp.zeros((length, half), F32)
    rest = jnp.zeros((length, HEAD_DIM - ROT), F32)
    keep = jnp.concatenate([cos, cos, rest + 1.0], axis=1)
    ahead = jnp.concatenate([-sin, zero, rest], axis=1)
    behind = jnp.concatenate([zero, sin, rest], axis=1)
    return tuple(jnp.concatenate([t, t], axis=1) for t in (keep, ahead, behind))


def turn(e, keep, ahead, behind):
    half = ROT // 2
    return e * keep + pltpu.roll(e, LANES - half, 1) * ahead + pltpu.roll(e, half, 1) * behind


def qkv_kernel(chunk, x_ref, w_ref, b_ref, keep_ref, ahead_ref, behind_ref, o_ref):
    def rows(i, _):
        at = pl.ds(pl.multiple_of(i * chunk, chunk), chunk)
        acc = jnp.dot(x_ref[at, :], w_ref[...], preferred_element_type=F32) + b_ref[...].astype(F32)
        keep, ahead, behind = keep_ref[at, :], ahead_ref[at, :], behind_ref[at, :]
        for g in range(acc.shape[1] // LANES):
            part = acc[:, g * LANES : (g + 1) * LANES]
            if g % 3 < 2:
                part = turn(part, keep, ahead, behind)
            o_ref[at, g * LANES : (g + 1) * LANES] = part.astype(BF16)
        return 0

    lax.fori_loop(0, x_ref.shape[0] // chunk, rows, 0)


def project(normed, w, b, tables):
    length, width = normed.shape
    cols = w.shape[1]
    tile = 768 if cols % 768 == 0 else 384
    const = lambda i: (0, 0)
    return pl.pallas_call(
        partial(qkv_kernel, min(512, length)),
        grid=(cols // tile,),
        in_specs=[
            pl.BlockSpec((length, width), const),
            pl.BlockSpec((width, tile), lambda i: (0, i)),
            pl.BlockSpec((1, tile), lambda i: (0, i)),
        ]
        + [pl.BlockSpec((length, LANES), const)] * 3,
        out_specs=pl.BlockSpec((length, tile), lambda i: (0, i)),
        out_shape=jax.ShapeDtypeStruct((length, cols), BF16),
        compiler_params=params(),
        cost_estimate=pl.CostEstimate(
            flops=2 * length * width * cols, bytes_accessed=2 * (length * width + width * cols + length * cols), transcendentals=0
        ),
        name="project",
    )(normed, w, b, *tables)


def nt(a, b):
    return lax.dot_general(a, b, (((1,), (1,)), ((), ())), preferred_element_type=F32)


def tn(a, b):
    return lax.dot_general(a, b, (((0,), (0,)), ((), ())), preferred_element_type=F32)


def attend_kernel(block, qkv_ref, o_ref, lse_ref, ka, va):
    length = qkv_ref.shape[0]
    lane = lax.broadcasted_iota(jnp.int32, (1, LANES), 1)
    scale = HEAD_DIM ** (-0.5)
    for h in range(2):
        mine = (lane < HEAD_DIM) if h == 0 else (lane >= HEAD_DIM)
        spare = HEAD_DIM if h == 0 else 0
        va[...] = jnp.where(mine, qkv_ref[:, 2 * LANES :], jnp.where(lane == spare, 1.0, 0.0).astype(BF16))
        for i in range(length // block):
            at = slice(i * block, (i + 1) * block)
            upto = (i + 1) * block
            q = jnp.where(mine, qkv_ref[at, :LANES] * jnp.asarray(scale, BF16), jnp.zeros((), BF16))
            diag = nt(q, qkv_ref[at, LANES : 2 * LANES])
            row = lax.broadcasted_iota(jnp.int32, (block, block), 0)
            col = lax.broadcasted_iota(jnp.int32, (block, block), 1)
            diag = jnp.where(row >= col, diag, MASKED)
            top = jnp.max(diag, axis=1, keepdims=True)
            if i:
                past = nt(q, qkv_ref[: i * block, LANES : 2 * LANES])
                top = jnp.maximum(top, jnp.max(past, axis=1, keepdims=True))
            acc = jnp.dot(jnp.exp(diag - top).astype(BF16), va[at, :], preferred_element_type=F32)
            if i:
                acc = acc + jnp.dot(
                    jnp.exp(past - top).astype(BF16), va[: i * block, :], preferred_element_type=F32
                )
            total = acc[:, spare : spare + 1]
            out = acc / total
            lse = jnp.broadcast_to(top + jnp.log(total), (block, LANES))
            if h == 0:
                o_ref[at, :] = out.astype(BF16)
                lse_ref[at, :] = lse
            else:
                o_ref[at, :] = jnp.where(mine, out.astype(BF16), o_ref[at, :])
                lse_ref[at, :] = jnp.where(mine, lse, lse_ref[at, :])


def attend(qkv, block=512):
    length, cols = qkv.shape
    pairs = cols // (3 * LANES)
    elements = pairs * length * length
    return pl.pallas_call(
        partial(attend_kernel, min(block, length)),
        grid=(pairs,),
        in_specs=[pl.BlockSpec((length, 3 * LANES), lambda i: (0, i))],
        out_specs=[pl.BlockSpec((length, LANES), lambda i: (0, i))] * 2,
        out_shape=[
            jax.ShapeDtypeStruct((length, pairs * LANES), BF16),
            jax.ShapeDtypeStruct((length, pairs * LANES), F32),
        ],
        scratch_shapes=[pltpu.VMEM((length, LANES), BF16)] * 2,
        compiler_params=params(),
        cost_estimate=pl.CostEstimate(
            flops=elements * 1024, bytes_accessed=12 * length * pairs * LANES, transcendentals=elements
        ),
        name="attend",
    )(qkv)


def split3(t):
    hi = t.astype(BF16)
    rest = t - hi.astype(F32)
    mid = rest.astype(BF16)
    return hi, mid, (rest - mid.astype(F32)).astype(BF16)


def grads_kernel(block, qkv_ref, do_ref, o_ref, lse_ref, keep_ref, ahead_ref, behind_ref, g_ref,
                 qa, ka, da, va, qm, km, dm, dq, dk, dv):
    length = qkv_ref.shape[0]
    count = length // block
    lane = lax.broadcasted_iota(jnp.int32, (1, LANES), 1)
    scale = HEAD_DIM ** (-0.5)
    zero = jnp.zeros((), BF16)
    dq[...] = jnp.zeros_like(dq)
    dk[...] = jnp.zeros_like(dk)
    dv[...] = jnp.zeros_like(dv)

    def augment(base, column, mine, spare):
        hi, mid, low = split3(column)
        extra = jnp.where(lane == spare, hi, jnp.where(lane == spare + 1, mid, jnp.where(lane == spare + 2, low, zero)))
        return jnp.where(mine, base, extra)

    for h in range(2):
        mine = (lane < HEAD_DIM) if h == 0 else (lane >= HEAD_DIM)
        spare = HEAD_DIM if h == 0 else 0
        own = 0 if h == 0 else HEAD_DIM
        ones = jnp.where((lane >= spare) & (lane < spare + 3), 1.0, 0.0).astype(BF16)

        def prepare(i, _):
            at = pl.ds(pl.multiple_of(i * block, block), block)
            q = qkv_ref[at, :LANES] * jnp.asarray(scale, BF16)
            k = qkv_ref[at, LANES : 2 * LANES]
            v = qkv_ref[at, 2 * LANES :]
            do = do_ref[at, :]
            product = jnp.where(mine, do.astype(F32) * o_ref[at, :].astype(F32), 0.0)
            delta = jnp.sum(product, axis=1, keepdims=True)
            lse = lse_ref[at, own : own + 1]
            qa[at, :] = augment(q, -lse, mine, spare)
            da[at, :] = augment(do, -delta, mine, spare)
            ka[at, :] = jnp.where(mine, k, ones)
            va[at, :] = jnp.where(mine, v, ones)
            qm[at, :] = jnp.where(mine, q, zero)
            km[at, :] = jnp.where(mine, k, zero)
            dm[at, :] = jnp.where(mine, do, zero)
            return 0

        lax.fori_loop(0, count, prepare, 0)

        def one(kat, qat, diagonal):
            scores = nt(ka[kat, :], qa[qat, :])
            if diagonal:
                key = lax.broadcasted_iota(jnp.int32, scores.shape, 0)
                query = lax.broadcasted_iota(jnp.int32, scores.shape, 1)
                scores = jnp.where(query >= key, scores, MASKED)
            weights = jnp.exp(scores)
            inner = nt(va[kat, :], da[qat, :])
            low = weights.astype(BF16)
            change = (weights * inner).astype(BF16)
            dv[kat, :] += jnp.dot(low, dm[qat, :], preferred_element_type=F32)
            dk[kat, :] += jnp.dot(change, qm[qat, :], preferred_element_type=F32)
            dq[qat, :] += tn(change, km[kat, :])

        def diagonal(j, _):
            at = pl.ds(pl.multiple_of(j * block, block), block)
            one(at, at, True)
            return 0

        lax.fori_loop(0, count, diagonal, 0)
        for j in range(count - 1):
            kat = slice(j * block, (j + 1) * block)

            def later(i, _):
                one(kat, pl.ds(pl.multiple_of(i * block, block), block), False)
                return 0

            lax.fori_loop(j + 1, count, later, 0)

    def finish(i, _):
        at = pl.ds(pl.multiple_of(i * block, block), block)
        keep, ahead, behind = keep_ref[at, :], -ahead_ref[at, :], -behind_ref[at, :]
        g_ref[at, :LANES] = turn(dq[at, :] * scale, keep, ahead, behind).astype(BF16)
        g_ref[at, LANES : 2 * LANES] = turn(dk[at, :], keep, ahead, behind).astype(BF16)
        g_ref[at, 2 * LANES :] = dv[at, :].astype(BF16)
        return 0

    lax.fori_loop(0, count, finish, 0)


def attend_grads(qkv, grad_mixed, mixed, lse, tables, block=512):
    length, cols = qkv.shape
    pairs = cols // (3 * LANES)
    elements = pairs * length * length
    const = lambda i: (0, 0)
    pair = pl.BlockSpec((length, LANES), lambda i: (0, i))
    return pl.pallas_call(
        partial(grads_kernel, min(block, length)),
        grid=(pairs,),
        in_specs=[pl.BlockSpec((length, 3 * LANES), lambda i: (0, i)), pair, pair, pair]
        + [pl.BlockSpec((length, LANES), const)] * 3,
        out_specs=pl.BlockSpec((length, 3 * LANES), lambda i: (0, i)),
        out_shape=jax.ShapeDtypeStruct((length, cols), BF16),
        scratch_shapes=[pltpu.VMEM((length, LANES), BF16)] * 7 + [pltpu.VMEM((length, LANES), F32)] * 3,
        compiler_params=params(),
        cost_estimate=pl.CostEstimate(
            flops=elements * 2560, bytes_accessed=20 * length * pairs * LANES, transcendentals=elements
        ),
        name="attend_grads",
    )(qkv, grad_mixed, mixed, lse, *tables)


def shard_pairs(size, flip):
    return [(s, s ^ flip) for s in range(size)]


def ring(size):
    return [(i, (i + 1) % size) for i in range(size)]


def pick(array, index, axis=0):
    return lax.dynamic_index_in_dim(array, index, axis, keepdims=False)


class Places:
    def __init__(self, mesh, batch):
        self.shard = mesh.shape["shard"]
        self.ctx = mesh.shape["ctx"]
        self.tensor = mesh.shape["tensor"]
        assert self.shard == 4 and self.ctx == 2 * (batch // self.shard)

    def locate(self):
        s = lax.axis_index("shard")
        self.s, self.z, self.y = s, lax.axis_index("ctx"), lax.axis_index("tensor")
        self.x, self.k = s // 2, s % 2

    def to_core(self, a):
        return lax.ppermute(a, "shard", shard_pairs(self.shard, 1))

    def to_x(self, a):
        return lax.ppermute(a, "shard", shard_pairs(self.shard, 2))

    def to_z(self, a):
        return lax.ppermute(a, "ctx", ring(self.ctx))

    def to_y(self, a):
        return lax.ppermute(a, "tensor", ring(self.tensor))

    def ordered(self, flag, first, second):
        return jnp.where(flag == 0, jnp.stack([first, second]), jnp.stack([second, first]))

    def rounds(self, turn):
        pairs = []
        for s in range(self.shard):
            x, c = s // 2, s % 2
            for z in range(self.ctx):
                target = (2 * x + z // 2) * self.ctx + 2 * c + (z + turn) % 2
                pairs.append((s * self.ctx + z, target))
        return pairs

    def spread(self, home):
        count, length, width = home.shape
        parts = home.reshape(count, self.tensor, length // self.tensor, width)
        got = []
        for turn in range(2):
            sent = parts[(self.z + turn) % 2, self.y]
            sent = jnp.where(self.x == 0, sent, jnp.roll(sent, width // 2, axis=1))
            got.append(lax.ppermute(sent, ("shard", "ctx"), self.rounds(turn)))
        return self.ordered(self.z % 2, got[0], got[1])

    def collect(self, pieces):
        got = []
        for turn in range(2):
            sent = pick(pieces, (self.z + turn) % 2)
            back = [(b, a) for a, b in self.rounds(turn)]
            got.append(lax.ppermute(sent, ("shard", "ctx"), back))
        home = self.ordered(self.z % 2, got[0], got[1])
        whole = self.join_y(home)
        whole = jnp.where(self.x == 0, whole, jnp.roll(whole, whole.shape[-1] // 2, axis=-1))
        return whole

    def join_y(self, pieces):
        count, rows, width = pieces.shape
        if self.tensor == 2:
            other = self.to_y(pieces)
            whole = jnp.where(
                self.y == 0, jnp.stack([pieces, other], axis=1), jnp.stack([other, pieces], axis=1)
            )
        else:
            whole = jnp.zeros((count, self.tensor, rows, width), pieces.dtype)
            current = pieces
            whole = lax.dynamic_update_index_in_dim(whole, current, self.y, 1)
            for step in range(self.tensor - 1):
                current = self.to_y(current)
                whole = lax.dynamic_update_index_in_dim(
                    whole, current, (self.y - 1 - step) % self.tensor, 1
                )
        return whole.reshape(count, self.tensor * rows, width)

    def join(self, pieces):
        half = self.join_y(pieces)
        half = half.reshape(-1, half.shape[-1])
        other = self.to_core(half)
        return self.ordered(self.k, half, other).reshape(2 * half.shape[0], half.shape[1])

    def sum_parts(self, part):
        rows, width = part.shape
        halves = part.reshape(2, rows // 2, width)
        got = self.to_core(pick(halves, 1 - self.k))
        mine = pick(halves, self.k).astype(F32) + got.astype(F32)
        mine = mine.reshape(2, self.tensor, rows // (4 * self.tensor), width)
        current = pick(mine, (self.y - 1) % self.tensor, 1)
        for step in range(self.tensor - 1):
            got = self.to_y(current.astype(BF16))
            current = pick(mine, (self.y - 2 - step) % self.tensor, 1) + got.astype(F32)
        return current

    def gather(self, local):
        rows, _, cols = local.shape
        got = self.to_core(pick(local, 1 - self.k, 1))
        block = self.ordered(self.k, pick(local, self.k, 1), got)
        held = jnp.zeros((2, self.ctx, rows, cols), local.dtype)
        held = lax.dynamic_update_index_in_dim(held, block, self.z, 1)
        for step in range(self.ctx - 1):
            block = self.to_z(block)
            held = lax.dynamic_update_index_in_dim(held, block, (self.z - 1 - step) % self.ctx, 1)
        held = held.reshape(-1, cols)
        return jnp.concatenate([held, self.to_x(held)])

    def scatter(self, rows_of, rows):
        sent = rows_of(1)
        got = self.to_x(sent)
        cols = sent.shape[1]
        total = (rows_of(0) + got.astype(F32)).astype(BF16).reshape(2, self.ctx, rows, cols)
        current = pick(total, (self.z - 1) % self.ctx, 1)
        for step in range(self.ctx - 1):
            got = self.to_z(current.astype(BF16))
            current = pick(total, (self.z - 2 - step) % self.ctx, 1).astype(F32) + got.astype(F32)
        got = self.to_core(pick(current, 1 - self.k))
        mine = pick(current, self.k)
        return jnp.where(
            self.k == 0, jnp.stack([mine, got], axis=1), jnp.stack([got, mine], axis=1)
        )


def shards(
    places, block_in, layer_norm_params, w_qkv, b_qkv, w_out, w_fc1, b_fc1, w_fc2, out_biases, cotangent
):
    places.locate()
    k = places.k
    seqs, local_len, width = block_in.shape
    length = local_len * places.ctx
    rows = w_qkv.shape[0]
    heads_width = w_qkv.shape[2]
    hidden_width = w_fc1.shape[1]
    pairs = heads_width // (2 * LANES)
    mixed_cols, hidden_cols = heads_width // 2, hidden_width // 2

    vectors = jnp.concatenate([layer_norm_params, out_biases]).T
    vectors = jnp.pad(vectors, ((0, 0), (0, LANES - 4)))
    local_out = jnp.concatenate(
        [w_out.T.reshape(rows, 2, mixed_cols), jnp.broadcast_to(vectors[:, None], (rows, 2, LANES))], axis=2
    )
    local_qkv = w_qkv.reshape(rows, 3, 2, pairs, LANES).transpose(0, 2, 3, 1, 4).reshape(rows, 2, 3 * mixed_cols)
    local_fc1 = w_fc1.reshape(rows, 2, hidden_cols)
    local_fc2 = w_fc2.T.reshape(rows, 2, hidden_cols)
    bias_qkv = pick(b_qkv.reshape(3, 2, pairs, LANES), k, 1).transpose(1, 0, 2).reshape(1, 3 * mixed_cols)
    bias_fc1 = pick(b_fc1.reshape(2, hidden_cols), k).astype(F32)

    x_pieces = places.spread(block_in)
    full_out = places.gather(local_out)
    full_qkv = places.gather(local_qkv)
    cot_pieces = places.spread(cotangent)
    full_fc1 = places.gather(local_fc1)
    full_fc2 = places.gather(local_fc2)

    row_vectors = full_out[:, mixed_cols : mixed_cols + 4].astype(F32).T
    gain, shift = row_vectors[0], row_vectors[1]
    full_out = full_out[:, :mixed_cols]

    inputs = x_pieces.astype(F32)
    average = jnp.mean(inputs, axis=-1, keepdims=True)
    centered = inputs - average
    variance = jnp.mean(centered * centered, axis=-1, keepdims=True)
    inverse = lax.rsqrt(variance + NORM_EPSILON)
    standard = centered * inverse
    normed = places.join((standard * gain + shift).astype(BF16))
    cot = places.join(cot_pieces)

    tables = rotation_tables(length)
    qkv = project(normed, full_qkv, bias_qkv, tables)
    mixed, lse = attend(qkv)
    grad_mixed = jnp.dot(cot, full_out, preferred_element_type=F32).astype(BF16)
    grad_qkv = attend_grads(qkv, grad_mixed, mixed, lse, tables)

    hidden_pre = jnp.dot(normed, full_fc1, preferred_element_type=F32) + bias_fc1
    activated, gelu_back = jax.vjp(partial(jax.nn.gelu, approximate=True), hidden_pre)
    hidden = activated.astype(BF16)
    grad_hidden = jnp.dot(cot, full_fc2, preferred_element_type=F32)
    grad_pre = gelu_back(grad_hidden)[0].astype(BF16)

    half = width // 2

    def rows_of(left, right):
        def part(which):
            out = tn(left[:, which * half : (which + 1) * half], right)
            return out.astype(BF16) if which else out
        return part

    grad_out = places.scatter(rows_of(cot, mixed), rows)
    grad_w_qkv = places.scatter(rows_of(normed, grad_qkv), rows)
    grad_fc2 = places.scatter(rows_of(cot, hidden), rows)
    grad_fc1 = places.scatter(rows_of(normed, grad_pre), rows)

    branches = nt(mixed, full_out) + nt(hidden, full_fc2)
    summed = places.sum_parts(branches.astype(BF16))
    result = (inputs + summed + row_vectors[2] + row_vectors[3]).astype(BF16)
    output = places.collect(result)

    grad_normed = nt(grad_qkv, full_qkv) + nt(grad_pre, full_fc1)
    grad_normed = places.sum_parts(grad_normed.astype(BF16))
    scaled = grad_normed * gain
    cot_rows = cot_pieces.astype(F32)
    grad_input = cot_rows + inverse * (
        scaled
        - jnp.mean(scaled, axis=-1, keepdims=True)
        - standard * jnp.mean(scaled * standard, axis=-1, keepdims=True)
    )
    grad_block = places.collect(grad_input.astype(BF16))

    sums = jnp.stack(
        [jnp.sum(grad_normed * standard, axis=(0, 1)), jnp.sum(grad_normed, axis=(0, 1)), jnp.sum(cot_rows, axis=(0, 1))]
    )
    sums = jnp.where(places.x == 0, sums, jnp.roll(sums, half, axis=1))
    grad_b_qkv = jnp.sum(grad_qkv.astype(F32), axis=0)
    grad_b_fc1 = jnp.sum(grad_pre.astype(F32), axis=0)
    packed = jnp.concatenate([sums.reshape(-1, LANES), grad_b_qkv.reshape(-1, LANES), grad_b_fc1.reshape(-1, LANES)])
    packed = packed + places.to_x(packed)
    hop = 1
    while hop < places.ctx:
        packed = packed + lax.ppermute(packed, "ctx", [(z, z ^ hop) for z in range(places.ctx)])
        hop *= 2
    other = places.to_core(packed)
    cut = 3 * width // LANES
    sums = packed[:cut] + other[:cut]
    hop = 1
    while hop < places.tensor:
        sums = sums + lax.ppermute(sums, "tensor", [(t, t ^ hop) for t in range(places.tensor)])
        hop *= 2
    sums = sums.reshape(3, width // LANES, LANES)
    mine = pick(sums, places.s * places.ctx + places.z, 1)
    halves = places.ordered(k, packed[cut:], other[cut:])
    grad_bqkv = halves[:, : 3 * pairs].reshape(2, pairs, 3, LANES).transpose(2, 0, 1, 3).reshape(3, heads_width)
    grad_bfc1 = halves[:, 3 * pairs :].reshape(hidden_width)

    grad_w_qkv = grad_w_qkv.reshape(rows, 2, pairs, 3, LANES).transpose(0, 3, 1, 2, 4).reshape(rows, 3, heads_width)
    return (
        output,
        grad_block,
        mine[:2],
        grad_w_qkv,
        grad_bqkv,
        grad_out.reshape(rows, heads_width).T,
        grad_fc1.reshape(rows, hidden_width),
        grad_bfc1,
        grad_fc2.reshape(rows, hidden_width).T,
        jnp.stack([mine[2], mine[2]]),
    )


def solution(mesh):
    split = ("shard", "ctx")
    in_specs = (
        P("shard", "ctx", None),
        P(None, split),
        P(split, None, "tensor"),
        P(None, "tensor"),
        P("tensor", split),
        P(split, "tensor"),
        P("tensor"),
        P("tensor", split),
        P(None, split),
        P("shard", "ctx", None),
    )
    out_specs = (
        P("shard", "ctx", None),
        P("shard", "ctx", None),
        P(None, split),
        P(split, None, "tensor"),
        P(None, "tensor"),
        P("tensor", split),
        P(split, "tensor"),
        P("tensor"),
        P("tensor", split),
        P(None, split),
    )

    def whole(*arrays):
        places = Places(mesh, arrays[0].shape[0])
        inner = jax.shard_map(
            partial(shards, places), mesh=mesh, in_specs=in_specs, out_specs=out_specs, check_vma=False
        )
        return inner(*arrays)

    return whole
```

```python
from functools import partial

import jax
import jax.numpy as jnp
from jax import lax
from jax.experimental import pallas as pl
from jax.experimental.pallas import tpu as pltpu
from jax.sharding import Mesh, PartitionSpec as P

HEAD_DIM = 64
ROT = 32
NORM_EPSILON = 1e-05
MASKED = -1000000000.0
LANES = 128
F32 = jnp.float32
BF16 = jnp.bfloat16
VMEM_LIMIT = 60 * 1024 * 1024
SMEM = pl.BlockSpec(memory_space=pltpu.SMEM)


def params(**kw):
    return pltpu.CompilerParams(vmem_limit_bytes=VMEM_LIMIT, **kw)


def cost(flops, moved, transcendentals=0):
    return pl.CostEstimate(flops=flops, bytes_accessed=moved, transcendentals=transcendentals)


def rotation_tables(length):
    half = ROT // 2
    frequency = 10000.0 ** (-(jnp.arange(half).astype(F32) * 2.0 / ROT))
    angles = jnp.arange(length).astype(F32)[:, None] * frequency[None, :]
    cos, sin = jnp.cos(angles), jnp.sin(angles)
    zero = jnp.zeros((length, half), F32)
    rest = jnp.zeros((length, HEAD_DIM - ROT), F32)
    keep = jnp.concatenate([cos, cos, rest + 1.0], axis=1)
    ahead = jnp.concatenate([-sin, zero, rest], axis=1)
    behind = jnp.concatenate([zero, sin, rest], axis=1)
    return tuple(jnp.concatenate([t, t], axis=1) for t in (keep, ahead, behind))


def turn(e, keep, ahead, behind):
    half = ROT // 2
    return e * keep + pltpu.roll(e, LANES - half, 1) * ahead + pltpu.roll(e, half, 1) * behind


def nt(a, b):
    return lax.dot_general(a, b, (((1,), (1,)), ((), ())), preferred_element_type=F32)


def tn(a, b):
    return lax.dot_general(a, b, (((0,), (0,)), ((), ())), preferred_element_type=F32)


def feature_block(position, ctx):
    x, z, core = position // (2 * ctx), position // 2 % ctx, position % 2
    return (x * 2 + core) * ctx + z


def token_block(place_ref, block):
    k = place_ref[1]
    return (block // 2 + k) % 2 * 2 + block % 2


def lanes(index):
    return slice(index * LANES, (index + 1) * LANES)


def norm_kernel(ctx, tensor, place_ref, vec_ref, *refs):
    o_ref = refs[-1]
    width = o_ref.shape[-1]
    for i, ref in enumerate(refs[:-1]):
        rows = ref[0].astype(F32)
        mean = jnp.mean(rows, axis=1, keepdims=True)
        centered = rows - mean
        inverse = lax.rsqrt(jnp.mean(centered * centered, axis=1, keepdims=True) + NORM_EPSILON)
        for p in range(width // LANES):
            at = slice(p * LANES, (p + 1) * LANES)
            part = ref[0, :, lanes(feature_block(p, ctx))].astype(F32)
            out = (part - mean) * inverse * vec_ref[0:1, at] + vec_ref[1:2, at]
            o_ref[i // tensor, 0, i % tensor, :, at] = out.astype(BF16)


def order_kernel(ctx, tensor, place_ref, *refs):
    o_ref = refs[-1]
    width = o_ref.shape[-1]
    for i, ref in enumerate(refs[:-1]):
        for p in range(width // LANES):
            at = slice(p * LANES, (p + 1) * LANES)
            o_ref[i // tensor, 0, i % tensor, :, at] = ref[0, :, lanes(feature_block(p, ctx))]


def arrange(kernel, name, places, place, pieces, extra=()):
    tensor = len(pieces) // 2
    _, rows, width = pieces[0].shape
    tile = max(rows // 2, 16)
    spec = pl.BlockSpec((1, tile, width), lambda b, t: (b, t, 0))
    out = pl.pallas_call(
        partial(kernel, places.ctx, tensor),
        grid=(2, rows // tile),
        in_specs=[SMEM] + [pl.BlockSpec(e.shape, lambda b, t: (0, 0)) for e in extra] + [spec] * len(pieces),
        out_specs=pl.BlockSpec((2, 1, tensor, tile, width), lambda b, t: (0, b, 0, t, 0)),
        out_shape=jax.ShapeDtypeStruct((2, 2, tensor, rows, width), BF16),
        compiler_params=params(),
        cost_estimate=cost(0, 8 * len(pieces) * rows * width),
        name=name,
    )(place, *extra, *pieces)
    return out.reshape(-1, width)


def project_kernel(tensor, place_ref, x_ref, w_ref, b_ref, keep_ref, ahead_ref, behind_ref, o_ref):
    block = x_ref.shape[0] // 4
    sub = block // tensor

    def rows(i, _):
        at = pl.ds(pl.multiple_of(i * block, block), block)
        acc = jnp.dot(x_ref[at, :], w_ref[...], preferred_element_type=F32) + b_ref[...].astype(F32)
        base = token_block(place_ref, i) * block
        for t in range(tensor):
            y = (place_ref[3] - t + tensor) % tensor
            to = pl.ds(pl.multiple_of(base + y * sub, sub), sub)
            keep, ahead, behind = keep_ref[to, :], ahead_ref[to, :], behind_ref[to, :]
            for g in range(acc.shape[1] // LANES):
                part = acc[t * sub : (t + 1) * sub, g * LANES : (g + 1) * LANES]
                if g % 3 < 2:
                    part = turn(part, keep, ahead, behind)
                o_ref[to, g * LANES : (g + 1) * LANES] = part.astype(BF16)
        return 0

    lax.fori_loop(0, 4, rows, 0)


def project(tensor, place, normed, w, cols, b, tables):
    length, width = normed.shape
    tile = 768 if cols % 768 == 0 else 384
    const = lambda i: (0, 0)
    return pl.pallas_call(
        partial(project_kernel, tensor),
        grid=(cols // tile,),
        in_specs=[
            SMEM,
            pl.BlockSpec((length, width), const),
            pl.BlockSpec((width, tile), lambda i: (0, i)),
            pl.BlockSpec((1, tile), lambda i: (0, i)),
        ]
        + [pl.BlockSpec((length, LANES), const)] * 3,
        out_specs=pl.BlockSpec((length, tile), lambda i: (0, i)),
        out_shape=jax.ShapeDtypeStruct((length, cols), BF16),
        compiler_params=params(),
        cost_estimate=cost(2 * length * width * cols, 2 * (length * width + width * cols + length * cols)),
        name="project",
    )(place, normed, w, b, *tables)


def attend_kernel(tensor, place_ref, qkv_ref, *refs):
    o_ref, lse_ref, va = refs[-3:]
    length = qkv_ref.shape[0]
    block = length // 4
    sub = block // tensor
    lane = lax.broadcasted_iota(jnp.int32, (1, LANES), 1)
    scale = HEAD_DIM ** (-0.5)
    mine = [lane < HEAD_DIM, lane >= HEAD_DIM]
    for h in range(2):
        spare = HEAD_DIM if h == 0 else 0
        va[h] = jnp.where(mine[h], qkv_ref[:, 2 * LANES :], jnp.where(lane == spare, 1.0, 0.0).astype(BF16))
    for i in range(4):
        at = slice(i * block, (i + 1) * block)
        outs, sums = [], []
        for h in range(2):
            spare = HEAD_DIM if h == 0 else 0
            q = jnp.where(mine[h], qkv_ref[at, :LANES] * jnp.asarray(scale, BF16), jnp.zeros((), BF16))
            diag = nt(q, qkv_ref[at, LANES : 2 * LANES])
            row = lax.broadcasted_iota(jnp.int32, (block, block), 0)
            col = lax.broadcasted_iota(jnp.int32, (block, block), 1)
            diag = jnp.where(row >= col, diag, MASKED)
            top = jnp.max(diag, axis=1, keepdims=True)
            if i:
                past = nt(q, qkv_ref[: i * block, LANES : 2 * LANES])
                top = jnp.maximum(top, jnp.max(past, axis=1, keepdims=True))
            acc = jnp.dot(jnp.exp(diag - top).astype(BF16), va[h, at, :], preferred_element_type=F32)
            if i:
                acc = acc + jnp.dot(
                    jnp.exp(past - top).astype(BF16), va[h, : i * block, :], preferred_element_type=F32
                )
            total = acc[:, spare : spare + 1]
            outs.append(acc / total)
            sums.append(jnp.broadcast_to(top + jnp.log(total), (block, LANES)))
        lse_ref[at, :] = jnp.where(mine[0], sums[0], sums[1])
        out = jnp.where(mine[0], outs[0], outs[1]).astype(BF16)
        base = token_block(place_ref, i) * block
        for y in range(tensor):
            back = (place_ref[3] - y + tensor) % tensor
            to = pl.ds(pl.multiple_of(base + back * sub, sub), sub)
            o_ref[to, :] = out[y * sub : (y + 1) * sub, :]


def attend(tensor, place, qkv, first, count, held=None):
    length, cols = qkv.shape
    pairs = cols // (3 * LANES)
    elements = count * length * length
    shapes = [
        jax.ShapeDtypeStruct((length, pairs * LANES), BF16),
        jax.ShapeDtypeStruct((length, pairs * LANES), F32),
    ]
    held = held or ()
    return pl.pallas_call(
        partial(attend_kernel, tensor),
        grid=(count,),
        in_specs=[SMEM, pl.BlockSpec((length, 3 * LANES), lambda i: (0, first + i))]
        + [pl.BlockSpec(memory_space=pl.ANY)] * len(held),
        out_specs=[pl.BlockSpec((length, LANES), lambda i: (0, first + i))] * 2,
        out_shape=shapes,
        scratch_shapes=[pltpu.VMEM((2, length, LANES), BF16)],
        input_output_aliases={2: 0, 3: 1} if held else {},
        compiler_params=params(),
        cost_estimate=cost(elements * 1024, 12 * length * count * LANES, elements),
        name="attend",
    )(place, qkv, *held)


def split3(t):
    hi = t.astype(BF16)
    rest = t - hi.astype(F32)
    mid = rest.astype(BF16)
    return hi, mid, (rest - mid.astype(F32)).astype(BF16)


def grads_kernel(tensor, place_ref, qkv_ref, do_ref, o_ref, lse_ref, keep_ref, ahead_ref, behind_ref, *refs):
    g_ref, qa, ka, da, va, qm, km, dm, dq, dk, dv = refs[-11:]
    length = qkv_ref.shape[0]
    count = 4
    block = length // count
    sub = block // tensor
    lane = lax.broadcasted_iota(jnp.int32, (1, LANES), 1)
    scale = HEAD_DIM ** (-0.5)
    zero = jnp.zeros((), BF16)
    dq[...] = jnp.zeros_like(dq)
    dk[...] = jnp.zeros_like(dk)
    dv[...] = jnp.zeros_like(dv)

    def augment(base, column, mine, spare):
        hi, mid, low = split3(column)
        extra = jnp.where(lane == spare, hi, jnp.where(lane == spare + 1, mid, jnp.where(lane == spare + 2, low, zero)))
        return jnp.where(mine, base, extra)

    def relative(i, y):
        back = (place_ref[3] - y + tensor) % tensor
        return pl.ds(pl.multiple_of(token_block(place_ref, i) * block + back * sub, sub), sub)

    for h in range(2):
        mine = (lane < HEAD_DIM) if h == 0 else (lane >= HEAD_DIM)
        spare = HEAD_DIM if h == 0 else 0
        own = 0 if h == 0 else HEAD_DIM
        ones = jnp.where((lane >= spare) & (lane < spare + 3), 1.0, 0.0).astype(BF16)

        def prepare(i, _):
            at = pl.ds(pl.multiple_of(i * block, block), block)
            q = qkv_ref[at, :LANES] * jnp.asarray(scale, BF16)
            k = qkv_ref[at, LANES : 2 * LANES]
            v = qkv_ref[at, 2 * LANES :]
            do = jnp.concatenate([do_ref[relative(i, y), :] for y in range(tensor)])
            o = jnp.concatenate([o_ref[relative(i, y), :] for y in range(tensor)])
            product = jnp.where(mine, do.astype(F32) * o.astype(F32), 0.0)
            delta = jnp.sum(product, axis=1, keepdims=True)
            lse = lse_ref[at, own : own + 1]
            qa[at, :] = augment(q, -lse, mine, spare)
            da[at, :] = augment(do, -delta, mine, spare)
            ka[at, :] = jnp.where(mine, k, ones)
            va[at, :] = jnp.where(mine, v, ones)
            qm[at, :] = jnp.where(mine, q, zero)
            km[at, :] = jnp.where(mine, k, zero)
            dm[at, :] = jnp.where(mine, do, zero)
            return 0

        lax.fori_loop(0, count, prepare, 0)

        def one(kat, qat, diagonal):
            scores = nt(ka[kat, :], qa[qat, :])
            if diagonal:
                key = lax.broadcasted_iota(jnp.int32, scores.shape, 0)
                query = lax.broadcasted_iota(jnp.int32, scores.shape, 1)
                scores = jnp.where(query >= key, scores, MASKED)
            weights = jnp.exp(scores)
            inner = nt(va[kat, :], da[qat, :])
            low = weights.astype(BF16)
            change = (weights * inner).astype(BF16)
            dv[kat, :] += jnp.dot(low, dm[qat, :], preferred_element_type=F32)
            dk[kat, :] += jnp.dot(change, qm[qat, :], preferred_element_type=F32)
            dq[qat, :] += tn(change, km[kat, :])

        def diagonal(j, _):
            at = pl.ds(pl.multiple_of(j * block, block), block)
            one(at, at, True)
            return 0

        lax.fori_loop(0, count, diagonal, 0)
        for j in range(count - 1):
            kat = slice(j * block, (j + 1) * block)

            def later(i, _):
                one(kat, pl.ds(pl.multiple_of(i * block, block), block), False)
                return 0

            lax.fori_loop(j + 1, count, later, 0)

    def finish(i, _):
        at = pl.ds(pl.multiple_of(i * block, block), block)
        keep, ahead, behind = keep_ref[at, :], -ahead_ref[at, :], -behind_ref[at, :]
        parts = (
            turn(dq[at, :] * scale, keep, ahead, behind).astype(BF16),
            turn(dk[at, :], keep, ahead, behind).astype(BF16),
            dv[at, :].astype(BF16),
        )
        for y in range(tensor):
            to = relative(i, y)
            for c in range(3):
                g_ref[to, c * LANES : (c + 1) * LANES] = parts[c][y * sub : (y + 1) * sub, :]
        return 0

    lax.fori_loop(0, count, finish, 0)


def attend_grads(tensor, place, qkv, grad_mixed, mixed, lse, tables, first, count, held=None):
    length, cols = qkv.shape
    elements = count * length * length
    const = lambda i: (0, 0)
    pair = pl.BlockSpec((length, LANES), lambda i: (0, first + i))
    triple = pl.BlockSpec((length, 3 * LANES), lambda i: (0, first + i))
    held = () if held is None else (held,)
    return pl.pallas_call(
        partial(grads_kernel, tensor),
        grid=(count,),
        in_specs=[SMEM, triple, pair, pair, pair]
        + [pl.BlockSpec((length, LANES), const)] * 3
        + [pl.BlockSpec(memory_space=pl.ANY)] * len(held),
        out_specs=triple,
        out_shape=jax.ShapeDtypeStruct((length, cols), BF16),
        scratch_shapes=[pltpu.VMEM((length, LANES), BF16)] * 7 + [pltpu.VMEM((length, LANES), F32)] * 3,
        input_output_aliases={8: 0} if held else {},
        compiler_params=params(),
        cost_estimate=cost(elements * 2560, 20 * length * count * LANES, elements),
        name="attend_grads",
    )(place, qkv, grad_mixed, mixed, lse, *tables, *held)


def finish_output_kernel(ctx, place_ref, vec_ref, x_ref, mine_ref, got_ref, o_ref):
    width = o_ref.shape[-1]
    for p in range(width // LANES):
        at = slice(p * LANES, (p + 1) * LANES)
        to = lanes(feature_block(p, ctx))
        total = mine_ref[:, at] + got_ref[:, at].astype(F32)
        out = x_ref[:, to].astype(F32) + total + vec_ref[2:3, at] + vec_ref[3:4, at]
        o_ref[:, to] = out.astype(BF16)


def finish_grads_kernel(ctx, place_ref, vec_ref, x_ref, cot_ref, mine_ref, got_ref, o_ref, sums_ref, xs, gs):
    width = o_ref.shape[-1]
    rows = x_ref[...].astype(F32)
    mean = jnp.mean(rows, axis=1, keepdims=True)
    centered = rows - mean
    inverse = lax.rsqrt(jnp.mean(centered * centered, axis=1, keepdims=True) + NORM_EPSILON)
    xs[...] = centered * inverse
    first = jnp.zeros_like(mean)
    second = jnp.zeros_like(mean)
    start = pl.program_id(0) == 0
    for p in range(width // LANES):
        at = slice(p * LANES, (p + 1) * LANES)
        to = lanes(feature_block(p, ctx))
        grad = mine_ref[:, at] + got_ref[:, at].astype(F32)
        standard = xs[:, to]
        scaled = grad * vec_ref[0:1, at]
        gs[:, to] = scaled
        first = first + jnp.sum(scaled, axis=1, keepdims=True)
        second = second + jnp.sum(scaled * standard, axis=1, keepdims=True)
        sums = jnp.concatenate(
            [
                jnp.sum(grad * standard, axis=0, keepdims=True),
                jnp.sum(grad, axis=0, keepdims=True),
                jnp.sum(cot_ref[:, to].astype(F32), axis=0, keepdims=True),
                jnp.zeros((5, LANES), F32),
            ]
        )
        sums_ref[:, to] = jnp.where(start, sums, sums_ref[:, to] + sums)
    out = cot_ref[...].astype(F32) + inverse * (gs[...] - first / width - xs[...] * (second / width))
    o_ref[...] = out.astype(BF16)


def finish(kernel, name, places, place, vectors, arrays, with_sums):
    rows, width = arrays[0].shape
    tile = min(128, rows)
    tiles = pl.BlockSpec((tile, width), lambda i: (i, 0))
    out_specs, out_shape = [tiles], [jax.ShapeDtypeStruct((rows, width), BF16)]
    if with_sums:
        out_specs.append(pl.BlockSpec((8, width), lambda i: (0, 0)))
        out_shape.append(jax.ShapeDtypeStruct((8, width), F32))
    return pl.pallas_call(
        partial(kernel, places.ctx),
        grid=(rows // tile,),
        in_specs=[SMEM, pl.BlockSpec(vectors.shape, lambda i: (0, 0))] + [tiles] * len(arrays),
        out_specs=out_specs,
        out_shape=out_shape,
        scratch_shapes=[pltpu.VMEM((tile, width), F32)] * 2 if with_sums else [],
        compiler_params=params(),
        cost_estimate=cost(0, 12 * rows * width),
        name=name,
    )(place, vectors, *arrays)


def assemble_kernel(tiles, cuts, place_ref, *refs):
    count = len(refs) - len(cuts)
    step = pl.program_id(0)
    for i, ref in enumerate(refs[:count]):

        @pl.when(step // tiles == i)
        def _(ref=ref):
            at = 0
            for o_ref, cols in zip(refs[count:], cuts):
                o_ref[...] = ref[:, at : at + cols]
                at += cols


def assemble(place, blocks, cuts):
    rows, cols = blocks[0].shape
    count = len(blocks)
    tile = min(256, rows)
    tiles = rows // tile

    def source(i):
        return lambda g, place_ref: (jnp.clip(g - i * tiles, 0, tiles - 1), 0)

    def target(g, place_ref):
        block = g // tiles
        other, step = block // 4, block % 4
        x = (place_ref[0] + other) % 2
        z = (place_ref[2] + 2 * (step % 2)) % 4
        z = z + (step // 2) * (1 - 2 * (z % 2))
        return ((x * 4 + z) * tiles + g % tiles, 0)

    return pl.pallas_call(
        partial(assemble_kernel, tiles, cuts),
        grid_spec=pltpu.PrefetchScalarGridSpec(
            num_scalar_prefetch=1,
            grid=(count * tiles,),
            in_specs=[pl.BlockSpec((tile, cols), source(i)) for i in range(count)],
            out_specs=[pl.BlockSpec((tile, cut), target) for cut in cuts],
        ),
        out_shape=[jax.ShapeDtypeStruct((count * rows, cut), BF16) for cut in cuts],
        compiler_params=params(),
        cost_estimate=cost(0, 4 * count * rows * cols),
        name="assemble",
    )(place, *blocks)


def ring(size):
    return [(i, (i + 1) % size) for i in range(size)]


def pick(array, index, axis=0):
    return lax.dynamic_index_in_dim(array, index, axis, keepdims=False)


def after(arrays, *landed):
    return lax.optimization_barrier((arrays, *landed))[0] if landed else arrays


class Places:
    def __init__(self, mesh, batch):
        self.ctx = mesh.shape["ctx"]
        self.tensor = mesh.shape["tensor"]
        assert mesh.shape["shard"] == 4 and self.ctx == 4 and batch == 8

    def locate(self):
        self.x, self.k = lax.axis_index("x"), lax.axis_index("core")
        self.z, self.y = lax.axis_index("ctx"), lax.axis_index("tensor")
        self.last = ()
        self.place = jnp.stack([self.x, self.k, self.z, self.y]).astype(jnp.int32)

    def to_core(self, a):
        return lax.ppermute(a, "core", [(0, 1), (1, 0)])

    def to_x(self, a):
        return lax.ppermute(a, "x", [(0, 1), (1, 0)])

    def stage(self, work, first, *rest, landed=()):
        out = work(after(first, *self.last, *landed), *rest)
        self.last = tuple(jax.tree.leaves(out))
        return out

    def pin(self, array):
        return after(array, *self.last)

    def to_z(self, a, hop):
        return lax.ppermute(a, "ctx", [(z, z ^ hop) for z in range(self.ctx)])

    def to_y(self, a):
        return lax.ppermute(a, "tensor", ring(self.tensor))

    def ordered(self, flag, first, second, axis=0):
        return jnp.where(
            flag == 0, jnp.stack([first, second], axis), jnp.stack([second, first], axis)
        )

    def rounds(self, turn):
        pairs = []
        for c in range(2):
            for z in range(self.ctx):
                pairs.append((c * self.ctx + z, z // 2 * self.ctx + 2 * c + (z + turn) % 2))
        return pairs

    def spread(self, home):
        count, length, width = home.shape
        parts = home.reshape(count, self.tensor, length // self.tensor, width)
        sent = [parts[(self.z + turn) % 2, self.y] for turn in range(2)]
        got = [lax.ppermute(sent[turn], ("core", "ctx"), self.rounds(turn)) for turn in range(2)]
        return self.ordered(self.z % 2, got[0], got[1])

    def collect(self, pieces):
        got = []
        for turn in range(2):
            sent = pick(pieces, (self.z + turn) % 2)
            back = [(b, a) for a, b in self.rounds(turn)]
            got.append(lax.ppermute(sent, ("core", "ctx"), back))
        return self.ordered(self.z % 2, got[0], got[1])

    def home(self, home):
        count, rows, width = home.shape
        if self.tensor == 2:
            whole = self.ordered(self.y, home, self.to_y(home), axis=1)
        else:
            whole = jnp.zeros((count, self.tensor, rows, width), home.dtype)
            current = home
            whole = lax.dynamic_update_index_in_dim(whole, current, self.y, 1)
            for step in range(self.tensor - 1):
                current = self.to_y(current)
                whole = lax.dynamic_update_index_in_dim(
                    whole, current, (self.y - 1 - step) % self.tensor, 1
                )
        return whole.reshape(count, self.tensor * rows, width)

    def pieces(self, own):
        mine = [own]
        theirs = [self.to_core(own)]
        for _ in range(self.tensor - 1):
            mine.append(self.to_y(mine[-1]))
            theirs.append(self.to_core(mine[-1]))
        return mine + theirs

    def swap(self, local):
        got = self.to_core(pick(local, 1 - self.k, 1))
        block = self.ordered(self.k, pick(local, self.k, 1), got)
        return block.reshape(-1, block.shape[-1])

    def core_parts(self, part):
        rows, width = part.shape
        halves = part.reshape(2, rows // 2, width)
        return halves[0], self.to_core(halves[1])

    def core_sum(self, mine, got):
        total = mine.astype(F32) + got.astype(F32)
        total = total.reshape(2, self.tensor, -1, total.shape[-1])
        return total[:, 0], total[:, 1 % self.tensor].astype(BF16), total

    def y_parts(self, sums):
        own, current, total = sums
        width = own.shape[-1]
        for step in range(self.tensor - 1):
            got = self.to_y(current)
            if step < self.tensor - 2:
                current = (total[:, 2 + step] + got.astype(F32)).astype(BF16)
        return own.reshape(-1, width), got.reshape(-1, width)

    def spread_core(self, sums):
        current = sums.reshape(2, -1, sums.shape[-1])
        got = self.to_core(pick(current, 1 - self.k))
        return self.ordered(self.k, pick(current, self.k), got, axis=1).astype(F32)

    def scatter(self, grad):
        return lax.psum_scatter(grad, ("x", "ctx"), scatter_dimension=0, tiled=True)

    def rows_x(self, grad, x):
        half = grad.shape[0] // 2
        return lax.dynamic_slice_in_dim(grad, x * half, half)

    def sum_x(self, grad, got):
        return (self.rows_x(grad, self.x).astype(F32) + got.astype(F32)).astype(BF16)

    def scatter_z(self, total):
        return lax.psum_scatter(total, "ctx", scatter_dimension=0, tiled=True)

    def gather(self, block):
        return lax.all_gather(block, ("x", "ctx"), axis=0, tiled=True)


def shards(
    places, block_in, layer_norm_params, w_qkv, b_qkv, w_out, w_fc1, b_fc1, w_fc2, out_biases, cotangent
):
    places.locate()
    k, place, tensor = places.k, places.place, places.tensor
    seqs, local_len, width = block_in.shape
    length = local_len * places.ctx
    rows = w_qkv.shape[0]
    heads_width = w_qkv.shape[2]
    hidden_width = w_fc1.shape[1]
    pairs = heads_width // (2 * LANES)
    mixed_cols, hidden_cols = heads_width // 2, hidden_width // 2
    qkv_cols = 3 * mixed_cols

    vectors = jnp.concatenate([layer_norm_params, out_biases]).T
    vectors = jnp.pad(vectors, ((0, 0), (0, LANES - 4)))
    local_a = jnp.concatenate(
        [
            w_qkv.reshape(rows, 3, 2, pairs, LANES).transpose(0, 2, 3, 1, 4).reshape(rows, 2, qkv_cols),
            w_out.T.reshape(rows, 2, mixed_cols),
            jnp.broadcast_to(vectors[:, None], (rows, 2, LANES)),
        ],
        axis=2,
    )
    bias_qkv = pick(b_qkv.reshape(3, 2, pairs, LANES), k, 1).transpose(1, 0, 2).reshape(1, qkv_cols)
    bias_fc1 = pick(b_fc1.reshape(2, hidden_cols), k).astype(F32)

    tables = rotation_tables(length)
    x_own = places.spread(block_in)
    a0 = places.swap(local_a)
    fc1_0 = places.swap(w_fc1.reshape(rows, 2, hidden_cols))
    fc2_0 = places.swap(w_fc2.T.reshape(rows, 2, hidden_cols))
    a0 = after(a0, fc1_0, fc2_0)
    a_first, a_second, a_x0 = places.to_z(a0, 2), places.to_z(a0, 1), places.to_x(a0)

    x_own, a_first, a_second, cotangent = after((x_own, a_first, a_second, cotangent), a_x0, *tables)
    cot_own = places.spread(cotangent)
    a_third, a_x1, a_x2 = places.to_z(a_first, 1), places.to_x(a_first), places.to_x(a_second)
    x_mine = [x_own]
    for _ in range(tensor - 1):
        x_mine.append(places.to_y(x_mine[-1]))

    a_third, cot_own, *x_mine = after((a_third, cot_own, *x_mine), a_x1, a_x2)
    full_fc1 = places.gather(after(fc1_0, a_third))
    a_x3 = places.to_x(a_third)
    x_theirs = [places.to_core(piece) for piece in x_mine]
    x_pieces = x_mine + x_theirs
    cot_mine, cot_theirs = [cot_own], []
    for _ in range(tensor - 1):
        cot_mine.append(places.to_y(cot_mine[-1]))
    a_blocks, a_x = [a0, a_first, a_second, a_third], [a_x0, a_x1, a_x2, a_x3]

    full_qkv, full_out, vectors = places.stage(
        lambda b: assemble(place, [b] + a_blocks[1:] + a_x, (qkv_cols, mixed_cols, LANES)), a0
    )
    full_fc2 = places.gather(places.pin(fc2_0))
    row_vectors = jnp.pad(vectors[:, :4].astype(F32).T, ((0, 4), (0, 0)))
    normed = places.stage(
        lambda p: arrange(norm_kernel, "norm", places, place, [p] + x_pieces[1:], (row_vectors,)), x_pieces[0]
    )
    qkv = places.stage(
        lambda n: project(tensor, place, n, full_qkv, qkv_cols, bias_qkv, tables), normed
    )
    step = max(1, pairs // 2)
    attended = places.stage(lambda a: attend(tensor, place, a, 0, step), qkv)
    cot_theirs += [places.to_core(places.pin(c)) for c in cot_mine]
    for first in range(step, pairs, step):
        attended = places.stage(
            lambda a: attend(tensor, place, a, first, step, attended), qkv, landed=tuple(cot_mine[1:])
        )
    mixed, lse = attended
    cot_pieces = cot_mine + cot_theirs
    cot = places.stage(
        lambda p: arrange(order_kernel, "order", places, place, [p] + cot_pieces[1:]), cot_pieces[0]
    )
    grad_mixed = places.stage(
        lambda c: jnp.dot(c, full_out, preferred_element_type=F32).astype(BF16), cot
    )
    def weight_grad(left, right):
        return places.stage(lambda a: tn(a, right).astype(BF16), left)

    def backward(first, grad_qkv):
        return places.stage(
            lambda g: attend_grads(tensor, place, qkv, g, mixed, lse, tables, first, 1, grad_qkv), grad_mixed
        )

    grad_w_out = places.scatter(weight_grad(cot, mixed))
    grad_qkv = None
    for first in range(pairs):
        grad_qkv = backward(first, grad_qkv)
    grad_w_qkv = places.scatter(weight_grad(normed, grad_qkv))

    def first_layer(n):
        pre = jnp.dot(n, full_fc1, preferred_element_type=F32) + bias_fc1
        out, back = jax.vjp(partial(jax.nn.gelu, approximate=True), pre)
        return out.astype(BF16), back(jnp.ones_like(pre))[0].astype(BF16)

    hidden, slope = places.stage(first_layer, normed)
    grad_fc2 = places.scatter(weight_grad(cot, hidden))
    branches = places.stage(
        lambda a: (nt(a, full_out) + nt(after(hidden, a), full_fc2)).astype(BF16), mixed
    )
    out_parts = places.core_parts(branches)

    def second_layer(c):
        grad_hidden = jnp.dot(c, full_fc2, preferred_element_type=F32)
        return (grad_hidden * slope.astype(F32)).astype(BF16)

    grad_pre = places.stage(second_layer, cot)
    out_mine, out_got = places.y_parts(places.stage(places.core_sum, *out_parts))
    grad_fc1 = weight_grad(normed, grad_pre)
    got_fc1 = places.to_x(places.stage(places.rows_x, grad_fc1, 1 - places.x))
    grad_normed = places.stage(
        lambda g: (nt(g, full_qkv) + nt(after(grad_pre, g), full_fc1)).astype(BF16), grad_qkv, landed=(out_got,)
    )
    grad_parts = places.core_parts(grad_normed)
    flat = lambda a: a.reshape(-1, width)
    (result,) = places.stage(
        lambda a: finish(
            finish_output_kernel, "finish_output", places, place, row_vectors, [a, out_mine, out_got], False
        ),
        flat(x_own),
    )
    out_home = places.collect(result.reshape(x_own.shape))
    grad_mine, grad_got = places.y_parts(places.stage(places.core_sum, *grad_parts))
    grad_in, sums = places.stage(
        lambda a: finish(
            finish_grads_kernel, "finish_grads", places, place, row_vectors,
            [a, flat(cot_own), grad_mine, grad_got], True,
        ),
        flat(x_own), landed=(out_home,),
    )
    grad_home = places.collect(grad_in.reshape(x_own.shape))
    grad_fc1 = places.scatter_z(places.stage(places.sum_x, grad_fc1, got_fc1))
    output = places.home(out_home)
    grad_block = places.home(grad_home)
    grad_w_out, grad_w_qkv, grad_fc2, grad_fc1 = after(
        (grad_w_out, grad_w_qkv, grad_fc2, grad_fc1), grad_in
    )
    grad_w_out = places.spread_core(grad_w_out)
    grad_w_qkv = places.spread_core(grad_w_qkv)
    grad_fc2 = places.spread_core(grad_fc2)
    grad_fc1 = places.spread_core(grad_fc1)

    grad_b_qkv = jnp.sum(grad_qkv.astype(F32), axis=0)
    grad_b_fc1 = jnp.sum(grad_pre.astype(F32), axis=0)
    packed = jnp.concatenate(
        [sums[:3].reshape(-1, LANES), grad_b_qkv.reshape(-1, LANES), grad_b_fc1.reshape(-1, LANES)]
    )
    packed = packed + places.to_x(packed)
    hop = 1
    while hop < places.ctx:
        packed = packed + places.to_z(packed, hop)
        hop *= 2
    other = places.to_core(packed)
    cut = 3 * width // LANES
    sums = packed[:cut] + other[:cut]
    hop = 1
    while hop < tensor:
        sums = sums + lax.ppermute(sums, "tensor", [(t, t ^ hop) for t in range(tensor)])
        hop *= 2
    sums = sums.reshape(3, width // LANES, LANES)
    mine = pick(sums, (places.x * 2 + k) * places.ctx + places.z, 1)
    halves = places.ordered(k, packed[cut:], other[cut:])
    grad_bqkv = halves[:, : 3 * pairs].reshape(2, pairs, 3, LANES).transpose(2, 0, 1, 3).reshape(3, heads_width)
    grad_bfc1 = halves[:, 3 * pairs :].reshape(hidden_width)

    grad_w_qkv = grad_w_qkv.reshape(rows, 2, pairs, 3, LANES)
    grad_w_qkv = grad_w_qkv.transpose(0, 3, 1, 2, 4).reshape(rows, 3, heads_width)
    grad_w_out = grad_w_out.reshape(rows, heads_width).T
    return (
        output,
        grad_block,
        mine[:2],
        grad_w_qkv,
        grad_bqkv,
        grad_w_out,
        grad_fc1.reshape(rows, hidden_width),
        grad_bfc1,
        grad_fc2.reshape(rows, hidden_width).T,
        jnp.stack([mine[2], mine[2]]),
    )


def solution(mesh):
    split = ("x", "core", "ctx")
    in_specs = (
        P(("x", "core"), "ctx", None),
        P(None, split),
        P(split, None, "tensor"),
        P(None, "tensor"),
        P("tensor", split),
        P(split, "tensor"),
        P("tensor"),
        P("tensor", split),
        P(None, split),
        P(("x", "core"), "ctx", None),
    )
    out_specs = (
        P(("x", "core"), "ctx", None),
        P(("x", "core"), "ctx", None),
        P(None, split),
        P(split, None, "tensor"),
        P(None, "tensor"),
        P("tensor", split),
        P(split, "tensor"),
        P("tensor"),
        P("tensor", split),
        P(None, split),
    )

    axes = (2, 2, mesh.shape["ctx"], mesh.shape["tensor"])
    fine = Mesh(mesh.devices.reshape(axes), ("x", "core", "ctx", "tensor"))

    def whole(*arrays):
        places = Places(mesh, arrays[0].shape[0])
        inner = jax.shard_map(
            partial(shards, places), mesh=fine, in_specs=in_specs, out_specs=out_specs, check_vma=False
        )
        return inner(*arrays)

    return whole
```

```python
from functools import partial

import jax
import jax.numpy as jnp
from jax import lax
from jax.experimental import pallas as pl
from jax.experimental.pallas import tpu as pltpu
from jax.sharding import Mesh, PartitionSpec as P

HEAD_DIM = 64
ROT = 32
NORM_EPSILON = 1e-05
MASKED = -1000000000.0
LANES = 128
F32 = jnp.float32
BF16 = jnp.bfloat16
VMEM_LIMIT = 60 * 1024 * 1024
SMEM = pl.BlockSpec(memory_space=pltpu.SMEM)


def params(**kw):
    return pltpu.CompilerParams(vmem_limit_bytes=VMEM_LIMIT, **kw)


def cost(flops, moved, transcendentals=0):
    return pl.CostEstimate(flops=flops, bytes_accessed=moved, transcendentals=transcendentals)


def rotation_tables(length):
    half = ROT // 2
    frequency = 10000.0 ** (-(jnp.arange(half).astype(F32) * 2.0 / ROT))
    angles = jnp.arange(length).astype(F32)[:, None] * frequency[None, :]
    cos, sin = jnp.cos(angles), jnp.sin(angles)
    zero = jnp.zeros((length, half), F32)
    rest = jnp.zeros((length, HEAD_DIM - ROT), F32)
    keep = jnp.concatenate([cos, cos, rest + 1.0], axis=1)
    ahead = jnp.concatenate([-sin, zero, rest], axis=1)
    behind = jnp.concatenate([zero, sin, rest], axis=1)
    return tuple(jnp.concatenate([t, t], axis=1) for t in (keep, ahead, behind))


def turn(e, keep, ahead, behind):
    half = ROT // 2
    return e * keep + pltpu.roll(e, LANES - half, 1) * ahead + pltpu.roll(e, half, 1) * behind


def nt(a, b):
    return lax.dot_general(a, b, (((1,), (1,)), ((), ())), preferred_element_type=F32)


def tn(a, b):
    return lax.dot_general(a, b, (((0,), (0,)), ((), ())), preferred_element_type=F32)


def feature_block(position, ctx):
    x, z, core = position // (2 * ctx), position // 2 % ctx, position % 2
    return (x * 2 + core) * ctx + z


def token_block(place_ref, block):
    k = place_ref[1]
    return (block // 2 + k) % 2 * 2 + block % 2


def lanes(index):
    return slice(index * LANES, (index + 1) * LANES)


def norm_kernel(ctx, tensor, place_ref, vec_ref, *refs):
    o_ref = refs[-1]
    width = o_ref.shape[-1]
    for i, ref in enumerate(refs[:-1]):
        rows = ref[0].astype(F32)
        mean = jnp.mean(rows, axis=1, keepdims=True)
        centered = rows - mean
        inverse = lax.rsqrt(jnp.mean(centered * centered, axis=1, keepdims=True) + NORM_EPSILON)
        for p in range(width // LANES):
            at = slice(p * LANES, (p + 1) * LANES)
            part = ref[0, :, lanes(feature_block(p, ctx))].astype(F32)
            out = (part - mean) * inverse * vec_ref[0:1, at] + vec_ref[1:2, at]
            o_ref[i // tensor, 0, i % tensor, :, at] = out.astype(BF16)


def order_kernel(ctx, tensor, place_ref, *refs):
    o_ref = refs[-1]
    width = o_ref.shape[-1]
    for i, ref in enumerate(refs[:-1]):
        for p in range(width // LANES):
            at = slice(p * LANES, (p + 1) * LANES)
            o_ref[i // tensor, 0, i % tensor, :, at] = ref[0, :, lanes(feature_block(p, ctx))]


def arrange(kernel, name, places, place, pieces, extra=()):
    tensor = len(pieces) // 2
    _, rows, width = pieces[0].shape
    tile = max(rows // 2, 16)
    spec = pl.BlockSpec((1, tile, width), lambda b, t: (b, t, 0))
    out = pl.pallas_call(
        partial(kernel, places.ctx, tensor),
        grid=(2, rows // tile),
        in_specs=[SMEM] + [pl.BlockSpec(e.shape, lambda b, t: (0, 0)) for e in extra] + [spec] * len(pieces),
        out_specs=pl.BlockSpec((2, 1, tensor, tile, width), lambda b, t: (0, b, 0, t, 0)),
        out_shape=jax.ShapeDtypeStruct((2, 2, tensor, rows, width), BF16),
        compiler_params=params(),
        cost_estimate=cost(0, 8 * len(pieces) * rows * width),
        name=name,
    )(place, *extra, *pieces)
    return out.reshape(-1, width)


def project_kernel(tensor, place_ref, x_ref, w_ref, b_ref, keep_ref, ahead_ref, behind_ref, o_ref):
    block = x_ref.shape[0] // 4
    sub = block // tensor

    def rows(i, _):
        at = pl.ds(pl.multiple_of(i * block, block), block)
        acc = jnp.dot(x_ref[at, :], w_ref[...], preferred_element_type=F32) + b_ref[...].astype(F32)
        base = token_block(place_ref, i) * block
        for t in range(tensor):
            y = (place_ref[3] - t + tensor) % tensor
            to = pl.ds(pl.multiple_of(base + y * sub, sub), sub)
            keep, ahead, behind = keep_ref[to, :], ahead_ref[to, :], behind_ref[to, :]
            for g in range(acc.shape[1] // LANES):
                part = acc[t * sub : (t + 1) * sub, g * LANES : (g + 1) * LANES]
                if g % 3 < 2:
                    part = turn(part, keep, ahead, behind)
                o_ref[to, g * LANES : (g + 1) * LANES] = part.astype(BF16)
        return 0

    lax.fori_loop(0, 4, rows, 0)


def project(tensor, place, normed, w, cols, b, tables):
    length, width = normed.shape
    tile = 768 if cols % 768 == 0 else 384
    const = lambda i: (0, 0)
    return pl.pallas_call(
        partial(project_kernel, tensor),
        grid=(cols // tile,),
        in_specs=[
            SMEM,
            pl.BlockSpec((length, width), const),
            pl.BlockSpec((width, tile), lambda i: (0, i)),
            pl.BlockSpec((1, tile), lambda i: (0, i)),
        ]
        + [pl.BlockSpec((length, LANES), const)] * 3,
        out_specs=pl.BlockSpec((length, tile), lambda i: (0, i)),
        out_shape=jax.ShapeDtypeStruct((length, cols), BF16),
        compiler_params=params(),
        cost_estimate=cost(2 * length * width * cols, 2 * (length * width + width * cols + length * cols)),
        name="project",
    )(place, normed, w, b, *tables)


def attend_kernel(tensor, place_ref, qkv_ref, *refs):
    o_ref, lse_ref, va = refs[-3:]
    length = qkv_ref.shape[0]
    block = length // 4
    sub = block // tensor
    lane = lax.broadcasted_iota(jnp.int32, (1, LANES), 1)
    scale = HEAD_DIM ** (-0.5)
    mine = [lane < HEAD_DIM, lane >= HEAD_DIM]
    for h in range(2):
        spare = HEAD_DIM if h == 0 else 0
        va[h] = jnp.where(mine[h], qkv_ref[:, 2 * LANES :], jnp.where(lane == spare, 1.0, 0.0).astype(BF16))
    for i in range(4):
        at = slice(i * block, (i + 1) * block)
        outs, sums = [], []
        for h in range(2):
            spare = HEAD_DIM if h == 0 else 0
            q = jnp.where(mine[h], qkv_ref[at, :LANES] * jnp.asarray(scale, BF16), jnp.zeros((), BF16))
            diag = nt(q, qkv_ref[at, LANES : 2 * LANES])
            row = lax.broadcasted_iota(jnp.int32, (block, block), 0)
            col = lax.broadcasted_iota(jnp.int32, (block, block), 1)
            diag = jnp.where(row >= col, diag, MASKED)
            top = jnp.max(diag, axis=1, keepdims=True)
            if i:
                past = nt(q, qkv_ref[: i * block, LANES : 2 * LANES])
                top = jnp.maximum(top, jnp.max(past, axis=1, keepdims=True))
            acc = jnp.dot(jnp.exp(diag - top).astype(BF16), va[h, at, :], preferred_element_type=F32)
            if i:
                acc = acc + jnp.dot(
                    jnp.exp(past - top).astype(BF16), va[h, : i * block, :], preferred_element_type=F32
                )
            total = acc[:, spare : spare + 1]
            outs.append(acc / total)
            sums.append(jnp.broadcast_to(top + jnp.log(total), (block, LANES)))
        lse_ref[at, :] = jnp.where(mine[0], sums[0], sums[1])
        out = jnp.where(mine[0], outs[0], outs[1]).astype(BF16)
        base = token_block(place_ref, i) * block
        for y in range(tensor):
            back = (place_ref[3] - y + tensor) % tensor
            to = pl.ds(pl.multiple_of(base + back * sub, sub), sub)
            o_ref[to, :] = out[y * sub : (y + 1) * sub, :]


def attend(tensor, place, qkv, first, count, held=None):
    length, cols = qkv.shape
    pairs = cols // (3 * LANES)
    elements = count * length * length
    shapes = [
        jax.ShapeDtypeStruct((length, pairs * LANES), BF16),
        jax.ShapeDtypeStruct((length, pairs * LANES), F32),
    ]
    held = held or ()
    return pl.pallas_call(
        partial(attend_kernel, tensor),
        grid=(count,),
        in_specs=[SMEM, pl.BlockSpec((length, 3 * LANES), lambda i: (0, first + i))]
        + [pl.BlockSpec(memory_space=pl.ANY)] * len(held),
        out_specs=[pl.BlockSpec((length, LANES), lambda i: (0, first + i))] * 2,
        out_shape=shapes,
        scratch_shapes=[pltpu.VMEM((2, length, LANES), BF16)],
        input_output_aliases={2: 0, 3: 1} if held else {},
        compiler_params=params(),
        cost_estimate=cost(elements * 1024, 12 * length * count * LANES, elements),
        name="attend",
    )(place, qkv, *held)


def split3(t):
    hi = t.astype(BF16)
    rest = t - hi.astype(F32)
    mid = rest.astype(BF16)
    return hi, mid, (rest - mid.astype(F32)).astype(BF16)


def grads_kernel(tensor, place_ref, qkv_ref, do_ref, o_ref, lse_ref, keep_ref, ahead_ref, behind_ref, *refs):
    g_ref, qa, ka, da, va, qm, km, dm, dq, dk, dv = refs[-11:]
    length = qkv_ref.shape[0]
    count = 4
    block = length // count
    sub = block // tensor
    lane = lax.broadcasted_iota(jnp.int32, (1, LANES), 1)
    scale = HEAD_DIM ** (-0.5)
    zero = jnp.zeros((), BF16)
    dq[...] = jnp.zeros_like(dq)
    dk[...] = jnp.zeros_like(dk)
    dv[...] = jnp.zeros_like(dv)

    def augment(base, column, mine, spare):
        hi, mid, low = split3(column)
        extra = jnp.where(lane == spare, hi, jnp.where(lane == spare + 1, mid, jnp.where(lane == spare + 2, low, zero)))
        return jnp.where(mine, base, extra)

    def relative(i, y):
        back = (place_ref[3] - y + tensor) % tensor
        return pl.ds(pl.multiple_of(token_block(place_ref, i) * block + back * sub, sub), sub)

    for h in range(2):
        mine = (lane < HEAD_DIM) if h == 0 else (lane >= HEAD_DIM)
        spare = HEAD_DIM if h == 0 else 0
        own = 0 if h == 0 else HEAD_DIM
        ones = jnp.where((lane >= spare) & (lane < spare + 3), 1.0, 0.0).astype(BF16)

        def prepare(i, _):
            at = pl.ds(pl.multiple_of(i * block, block), block)
            q = qkv_ref[at, :LANES] * jnp.asarray(scale, BF16)
            k = qkv_ref[at, LANES : 2 * LANES]
            v = qkv_ref[at, 2 * LANES :]
            do = jnp.concatenate([do_ref[relative(i, y), :] for y in range(tensor)])
            o = jnp.concatenate([o_ref[relative(i, y), :] for y in range(tensor)])
            product = jnp.where(mine, do.astype(F32) * o.astype(F32), 0.0)
            delta = jnp.sum(product, axis=1, keepdims=True)
            lse = lse_ref[at, own : own + 1]
            qa[at, :] = augment(q, -lse, mine, spare)
            da[at, :] = augment(do, -delta, mine, spare)
            ka[at, :] = jnp.where(mine, k, ones)
            va[at, :] = jnp.where(mine, v, ones)
            qm[at, :] = jnp.where(mine, q, zero)
            km[at, :] = jnp.where(mine, k, zero)
            dm[at, :] = jnp.where(mine, do, zero)
            return 0

        lax.fori_loop(0, count, prepare, 0)

        def one(kat, qat, diagonal):
            scores = nt(ka[kat, :], qa[qat, :])
            if diagonal:
                key = lax.broadcasted_iota(jnp.int32, scores.shape, 0)
                query = lax.broadcasted_iota(jnp.int32, scores.shape, 1)
                scores = jnp.where(query >= key, scores, MASKED)
            weights = jnp.exp(scores)
            inner = nt(va[kat, :], da[qat, :])
            low = weights.astype(BF16)
            change = (weights * inner).astype(BF16)
            dv[kat, :] += jnp.dot(low, dm[qat, :], preferred_element_type=F32)
            dk[kat, :] += jnp.dot(change, qm[qat, :], preferred_element_type=F32)
            dq[qat, :] += tn(change, km[kat, :])

        def diagonal(j, _):
            at = pl.ds(pl.multiple_of(j * block, block), block)
            one(at, at, True)
            return 0

        lax.fori_loop(0, count, diagonal, 0)
        for j in range(count - 1):
            kat = slice(j * block, (j + 1) * block)

            def later(i, _):
                one(kat, pl.ds(pl.multiple_of(i * block, block), block), False)
                return 0

            lax.fori_loop(j + 1, count, later, 0)

    def finish(i, _):
        at = pl.ds(pl.multiple_of(i * block, block), block)
        keep, ahead, behind = keep_ref[at, :], -ahead_ref[at, :], -behind_ref[at, :]
        parts = (
            turn(dq[at, :] * scale, keep, ahead, behind).astype(BF16),
            turn(dk[at, :], keep, ahead, behind).astype(BF16),
            dv[at, :].astype(BF16),
        )
        for y in range(tensor):
            to = relative(i, y)
            for c in range(3):
                g_ref[to, c * LANES : (c + 1) * LANES] = parts[c][y * sub : (y + 1) * sub, :]
        return 0

    lax.fori_loop(0, count, finish, 0)


def attend_grads(tensor, place, qkv, grad_mixed, mixed, lse, tables, first, count, held=None):
    length, cols = qkv.shape
    elements = count * length * length
    const = lambda i: (0, 0)
    pair = pl.BlockSpec((length, LANES), lambda i: (0, first + i))
    triple = pl.BlockSpec((length, 3 * LANES), lambda i: (0, first + i))
    held = () if held is None else (held,)
    return pl.pallas_call(
        partial(grads_kernel, tensor),
        grid=(count,),
        in_specs=[SMEM, triple, pair, pair, pair]
        + [pl.BlockSpec((length, LANES), const)] * 3
        + [pl.BlockSpec(memory_space=pl.ANY)] * len(held),
        out_specs=triple,
        out_shape=jax.ShapeDtypeStruct((length, cols), BF16),
        scratch_shapes=[pltpu.VMEM((length, LANES), BF16)] * 7 + [pltpu.VMEM((length, LANES), F32)] * 3,
        input_output_aliases={8: 0} if held else {},
        compiler_params=params(),
        cost_estimate=cost(elements * 2560, 20 * length * count * LANES, elements),
        name="attend_grads",
    )(place, qkv, grad_mixed, mixed, lse, *tables, *held)


def finish_output_kernel(ctx, place_ref, vec_ref, x_ref, mine_ref, got_ref, o_ref):
    width = o_ref.shape[-1]
    for p in range(width // LANES):
        at = slice(p * LANES, (p + 1) * LANES)
        to = lanes(feature_block(p, ctx))
        total = mine_ref[:, at] + got_ref[:, at].astype(F32)
        out = x_ref[:, to].astype(F32) + total + vec_ref[2:3, at] + vec_ref[3:4, at]
        o_ref[:, to] = out.astype(BF16)


def finish_grads_kernel(ctx, place_ref, vec_ref, x_ref, cot_ref, mine_ref, got_ref, o_ref, sums_ref, xs, gs):
    width = o_ref.shape[-1]
    rows = x_ref[...].astype(F32)
    mean = jnp.mean(rows, axis=1, keepdims=True)
    centered = rows - mean
    inverse = lax.rsqrt(jnp.mean(centered * centered, axis=1, keepdims=True) + NORM_EPSILON)
    xs[...] = centered * inverse
    first = jnp.zeros_like(mean)
    second = jnp.zeros_like(mean)
    start = pl.program_id(0) == 0
    for p in range(width // LANES):
        at = slice(p * LANES, (p + 1) * LANES)
        to = lanes(feature_block(p, ctx))
        grad = mine_ref[:, at] + got_ref[:, at].astype(F32)
        standard = xs[:, to]
        scaled = grad * vec_ref[0:1, at]
        gs[:, to] = scaled
        first = first + jnp.sum(scaled, axis=1, keepdims=True)
        second = second + jnp.sum(scaled * standard, axis=1, keepdims=True)
        sums = jnp.concatenate(
            [
                jnp.sum(grad * standard, axis=0, keepdims=True),
                jnp.sum(grad, axis=0, keepdims=True),
                jnp.sum(cot_ref[:, to].astype(F32), axis=0, keepdims=True),
                jnp.zeros((5, LANES), F32),
            ]
        )
        sums_ref[:, to] = jnp.where(start, sums, sums_ref[:, to] + sums)
    out = cot_ref[...].astype(F32) + inverse * (gs[...] - first / width - xs[...] * (second / width))
    o_ref[...] = out.astype(BF16)


def finish(kernel, name, places, place, vectors, arrays, with_sums):
    rows, width = arrays[0].shape
    tile = min(128, rows)
    tiles = pl.BlockSpec((tile, width), lambda i: (i, 0))
    out_specs, out_shape = [tiles], [jax.ShapeDtypeStruct((rows, width), BF16)]
    if with_sums:
        out_specs.append(pl.BlockSpec((8, width), lambda i: (0, 0)))
        out_shape.append(jax.ShapeDtypeStruct((8, width), F32))
    return pl.pallas_call(
        partial(kernel, places.ctx),
        grid=(rows // tile,),
        in_specs=[SMEM, pl.BlockSpec(vectors.shape, lambda i: (0, 0))] + [tiles] * len(arrays),
        out_specs=out_specs,
        out_shape=out_shape,
        scratch_shapes=[pltpu.VMEM((tile, width), F32)] * 2 if with_sums else [],
        compiler_params=params(),
        cost_estimate=cost(0, 12 * rows * width),
        name=name,
    )(place, vectors, *arrays)


def assemble_kernel(tiles, cuts, place_ref, *refs):
    count = len(refs) - len(cuts)
    step = pl.program_id(0)
    for i, ref in enumerate(refs[:count]):

        @pl.when(step // tiles == i)
        def _(ref=ref):
            at = 0
            for o_ref, cols in zip(refs[count:], cuts):
                o_ref[...] = ref[:, at : at + cols]
                at += cols


def assemble(place, blocks, cuts):
    rows, cols = blocks[0].shape
    count = len(blocks)
    tile = min(256, rows)
    tiles = rows // tile

    def source(i):
        return lambda g, place_ref: (jnp.clip(g - i * tiles, 0, tiles - 1), 0)

    def target(g, place_ref):
        block = g // tiles
        other, step = block // 4, block % 4
        x = (place_ref[0] + other) % 2
        z = (place_ref[2] + 2 * (step % 2)) % 4
        z = z + (step // 2) * (1 - 2 * (z % 2))
        return ((x * 4 + z) * tiles + g % tiles, 0)

    return pl.pallas_call(
        partial(assemble_kernel, tiles, cuts),
        grid_spec=pltpu.PrefetchScalarGridSpec(
            num_scalar_prefetch=1,
            grid=(count * tiles,),
            in_specs=[pl.BlockSpec((tile, cols), source(i)) for i in range(count)],
            out_specs=[pl.BlockSpec((tile, cut), target) for cut in cuts],
        ),
        out_shape=[jax.ShapeDtypeStruct((count * rows, cut), BF16) for cut in cuts],
        compiler_params=params(),
        cost_estimate=cost(0, 4 * count * rows * cols),
        name="assemble",
    )(place, *blocks)


def ring(size):
    return [(i, (i + 1) % size) for i in range(size)]


def pick(array, index, axis=0):
    return lax.dynamic_index_in_dim(array, index, axis, keepdims=False)


def after(arrays, *landed):
    return lax.optimization_barrier((arrays, *landed))[0] if landed else arrays


class Places:
    def __init__(self, mesh, batch):
        self.ctx = mesh.shape["ctx"]
        self.tensor = mesh.shape["tensor"]
        assert mesh.shape["shard"] == 4 and self.ctx == 4 and batch == 8

    def locate(self):
        self.x, self.k = lax.axis_index("x"), lax.axis_index("core")
        self.z, self.y = lax.axis_index("ctx"), lax.axis_index("tensor")
        self.last = ()
        self.place = jnp.stack([self.x, self.k, self.z, self.y]).astype(jnp.int32)

    def to_core(self, a):
        return lax.ppermute(a, "core", [(0, 1), (1, 0)])

    def to_x(self, a):
        return lax.ppermute(a, "x", [(0, 1), (1, 0)])

    def stage(self, work, first, *rest, landed=()):
        out = work(after(first, *self.last, *landed), *rest)
        self.last = tuple(jax.tree.leaves(out))
        return out

    def pin(self, array):
        return after(array, *self.last)

    def to_z(self, a, hop):
        return lax.ppermute(a, "ctx", [(z, z ^ hop) for z in range(self.ctx)])

    def to_y(self, a):
        return lax.ppermute(a, "tensor", ring(self.tensor))

    def ordered(self, flag, first, second, axis=0):
        return jnp.where(
            flag == 0, jnp.stack([first, second], axis), jnp.stack([second, first], axis)
        )

    def rounds(self, turn):
        pairs = []
        for c in range(2):
            for z in range(self.ctx):
                pairs.append((c * self.ctx + z, z // 2 * self.ctx + 2 * c + (z + turn) % 2))
        return pairs

    def spread(self, home):
        count, length, width = home.shape
        parts = home.reshape(count, self.tensor, length // self.tensor, width)
        sent = [parts[(self.z + turn) % 2, self.y] for turn in range(2)]
        got = [lax.ppermute(sent[turn], ("core", "ctx"), self.rounds(turn)) for turn in range(2)]
        return self.ordered(self.z % 2, got[0], got[1])

    def collect(self, pieces):
        got = []
        for turn in range(2):
            sent = pick(pieces, (self.z + turn) % 2)
            back = [(b, a) for a, b in self.rounds(turn)]
            got.append(lax.ppermute(sent, ("core", "ctx"), back))
        return self.ordered(self.z % 2, got[0], got[1])

    def home(self, home):
        count, rows, width = home.shape
        if self.tensor == 2:
            whole = self.ordered(self.y, home, self.to_y(home), axis=1)
        else:
            whole = jnp.zeros((count, self.tensor, rows, width), home.dtype)
            current = home
            whole = lax.dynamic_update_index_in_dim(whole, current, self.y, 1)
            for step in range(self.tensor - 1):
                current = self.to_y(current)
                whole = lax.dynamic_update_index_in_dim(
                    whole, current, (self.y - 1 - step) % self.tensor, 1
                )
        return whole.reshape(count, self.tensor * rows, width)

    def pieces(self, own):
        mine = [own]
        theirs = [self.to_core(own)]
        for _ in range(self.tensor - 1):
            mine.append(self.to_y(mine[-1]))
            theirs.append(self.to_core(mine[-1]))
        return mine + theirs

    def swap(self, local):
        got = self.to_core(pick(local, 1 - self.k, 1))
        block = self.ordered(self.k, pick(local, self.k, 1), got)
        return block.reshape(-1, block.shape[-1])

    def core_parts(self, part):
        rows, width = part.shape
        halves = part.reshape(2, rows // 2, width)
        return halves[0], self.to_core(halves[1])

    def core_sum(self, mine, got):
        total = mine.astype(F32) + got.astype(F32)
        total = total.reshape(2, self.tensor, -1, total.shape[-1])
        return total[:, 0], total[:, 1 % self.tensor].astype(BF16), total

    def y_parts(self, sums):
        own, current, total = sums
        width = own.shape[-1]
        for step in range(self.tensor - 1):
            got = self.to_y(current)
            if step < self.tensor - 2:
                current = (total[:, 2 + step] + got.astype(F32)).astype(BF16)
        return own.reshape(-1, width), got.reshape(-1, width)

    def spread_core(self, sums):
        current = sums.reshape(2, -1, sums.shape[-1])
        got = self.to_core(pick(current, 1 - self.k))
        return self.ordered(self.k, pick(current, self.k), got, axis=1).astype(F32)

    def scatter(self, grad):
        return lax.psum_scatter(grad, ("x", "ctx"), scatter_dimension=0, tiled=True)

    def rows_x(self, grad, x):
        half = grad.shape[0] // 2
        return lax.dynamic_slice_in_dim(grad, x * half, half)

    def sum_x(self, grad, got):
        return (self.rows_x(grad, self.x).astype(F32) + got.astype(F32)).astype(BF16)

    def scatter_z(self, total):
        return lax.psum_scatter(total, "ctx", scatter_dimension=0, tiled=True)

    def gather(self, block):
        return lax.all_gather(block, ("x", "ctx"), axis=0, tiled=True)


def shards(
    places, block_in, layer_norm_params, w_qkv, b_qkv, w_out, w_fc1, b_fc1, w_fc2, out_biases, cotangent
):
    places.locate()
    k, place, tensor = places.k, places.place, places.tensor
    seqs, local_len, width = block_in.shape
    length = local_len * places.ctx
    rows = w_qkv.shape[0]
    heads_width = w_qkv.shape[2]
    hidden_width = w_fc1.shape[1]
    pairs = heads_width // (2 * LANES)
    mixed_cols, hidden_cols = heads_width // 2, hidden_width // 2
    qkv_cols = 3 * mixed_cols

    vectors = jnp.concatenate([layer_norm_params, out_biases]).T
    vectors = jnp.pad(vectors, ((0, 0), (0, LANES - 4)))
    local_a = jnp.concatenate(
        [
            w_qkv.reshape(rows, 3, 2, pairs, LANES).transpose(0, 2, 3, 1, 4).reshape(rows, 2, qkv_cols),
            w_out.T.reshape(rows, 2, mixed_cols),
            jnp.broadcast_to(vectors[:, None], (rows, 2, LANES)),
        ],
        axis=2,
    )
    bias_qkv = pick(b_qkv.reshape(3, 2, pairs, LANES), k, 1).transpose(1, 0, 2).reshape(1, qkv_cols)
    bias_fc1 = pick(b_fc1.reshape(2, hidden_cols), k).astype(F32)

    tables = rotation_tables(length)
    x_own = places.spread(block_in)
    a0 = places.swap(local_a)
    fc1_0 = places.swap(w_fc1.reshape(rows, 2, hidden_cols))
    fc2_0 = places.swap(w_fc2.T.reshape(rows, 2, hidden_cols))
    a0 = after(a0, fc1_0, fc2_0)
    a_first, a_second, a_x0 = places.to_z(a0, 2), places.to_z(a0, 1), places.to_x(a0)

    x_own, a_first, a_second, cotangent = after((x_own, a_first, a_second, cotangent), a_x0, *tables)
    cot_own = places.spread(cotangent)
    a_third, a_x1, a_x2 = places.to_z(a_first, 1), places.to_x(a_first), places.to_x(a_second)
    x_mine = [x_own]
    for _ in range(tensor - 1):
        x_mine.append(places.to_y(x_mine[-1]))

    a_third, cot_own, *x_mine = after((a_third, cot_own, *x_mine), a_x1, a_x2)
    full_fc1 = places.gather(after(fc1_0, a_third))
    a_x3 = places.to_x(a_third)
    x_theirs = [places.to_core(piece) for piece in x_mine]
    x_pieces = x_mine + x_theirs
    cot_mine, cot_theirs = [cot_own], []
    for _ in range(tensor - 1):
        cot_mine.append(places.to_y(cot_mine[-1]))
    a_blocks, a_x = [a0, a_first, a_second, a_third], [a_x0, a_x1, a_x2, a_x3]

    full_qkv, full_out, vectors = places.stage(
        lambda b: assemble(place, [b] + a_blocks[1:] + a_x, (qkv_cols, mixed_cols, LANES)), a0
    )
    full_fc2 = places.gather(places.pin(fc2_0))
    row_vectors = jnp.pad(vectors[:, :4].astype(F32).T, ((0, 4), (0, 0)))
    normed = places.stage(
        lambda p: arrange(norm_kernel, "norm", places, place, [p] + x_pieces[1:], (row_vectors,)), x_pieces[0]
    )
    qkv = places.stage(
        lambda n: project(tensor, place, n, full_qkv, qkv_cols, bias_qkv, tables), normed
    )
    step = max(1, pairs // 2)
    attended = places.stage(lambda a: attend(tensor, place, a, 0, step), qkv)
    cot_theirs += [places.to_core(places.pin(c)) for c in cot_mine]
    for first in range(step, pairs, step):
        attended = places.stage(
            lambda a: attend(tensor, place, a, first, step, attended), qkv, landed=tuple(cot_mine[1:])
        )
    mixed, lse = attended
    cot_pieces = cot_mine + cot_theirs
    cot = places.stage(
        lambda p: arrange(order_kernel, "order", places, place, [p] + cot_pieces[1:]), cot_pieces[0]
    )
    grad_mixed = places.stage(
        lambda c: jnp.dot(c, full_out, preferred_element_type=F32).astype(BF16), cot
    )
    def weight_grad(left, right):
        return places.stage(lambda a: tn(a, right).astype(BF16), left)

    def backward(first, grad_qkv):
        return places.stage(
            lambda g: attend_grads(tensor, place, qkv, g, mixed, lse, tables, first, 1, grad_qkv), grad_mixed
        )

    grad_w_out = places.scatter(weight_grad(cot, mixed))
    grad_qkv = None
    for first in range(pairs):
        grad_qkv = backward(first, grad_qkv)
    grad_w_qkv = places.scatter(weight_grad(normed, grad_qkv))

    def first_layer(n):
        pre = jnp.dot(n, full_fc1, preferred_element_type=F32) + bias_fc1
        out, back = jax.vjp(partial(jax.nn.gelu, approximate=True), pre)
        return out.astype(BF16), back(jnp.ones_like(pre))[0].astype(BF16)

    hidden, slope = places.stage(first_layer, normed)
    grad_fc2 = places.scatter(weight_grad(cot, hidden))
    branches = places.stage(
        lambda a: (nt(a, full_out) + nt(after(hidden, a), full_fc2)).astype(BF16), mixed
    )
    out_parts = places.core_parts(branches)

    def second_layer(c):
        grad_hidden = jnp.dot(c, full_fc2, preferred_element_type=F32)
        return (grad_hidden * slope.astype(F32)).astype(BF16)

    grad_pre = places.stage(second_layer, cot)
    out_mine, out_got = places.y_parts(places.stage(places.core_sum, *out_parts))
    grad_fc1 = weight_grad(normed, grad_pre)
    got_fc1 = places.to_x(places.stage(places.rows_x, grad_fc1, 1 - places.x))
    grad_normed = places.stage(
        lambda g: (nt(g, full_qkv) + nt(after(grad_pre, g), full_fc1)).astype(BF16), grad_qkv, landed=(out_got,)
    )
    grad_parts = places.core_parts(grad_normed)
    flat = lambda a: a.reshape(-1, width)
    (result,) = places.stage(
        lambda a: finish(
            finish_output_kernel, "finish_output", places, place, row_vectors, [a, out_mine, out_got], False
        ),
        flat(x_own),
    )
    out_home = places.collect(result.reshape(x_own.shape))
    grad_mine, grad_got = places.y_parts(places.stage(places.core_sum, *grad_parts))
    grad_in, sums = places.stage(
        lambda a: finish(
            finish_grads_kernel, "finish_grads", places, place, row_vectors,
            [a, flat(cot_own), grad_mine, grad_got], True,
        ),
        flat(x_own), landed=(out_home,),
    )
    grad_home = places.collect(grad_in.reshape(x_own.shape))
    grad_fc1 = places.scatter_z(
        places.stage(places.sum_x, grad_fc1, got_fc1, landed=(grad_home,))
    )
    output = places.home(out_home)
    grad_block = places.home(grad_home)
    grad_w_out, grad_w_qkv, grad_fc2 = after((grad_w_out, grad_w_qkv, grad_fc2), grad_home)
    grad_w_out = places.spread_core(grad_w_out)
    grad_w_qkv = places.spread_core(grad_w_qkv)
    grad_fc2 = places.spread_core(grad_fc2)
    grad_fc1 = places.spread_core(grad_fc1)

    sums = after(sums, output, grad_block)
    grad_b_qkv = jnp.sum(grad_qkv.astype(F32), axis=0)
    grad_b_fc1 = jnp.sum(grad_pre.astype(F32), axis=0)
    packed = jnp.concatenate(
        [sums[:3].reshape(-1, LANES), grad_b_qkv.reshape(-1, LANES), grad_b_fc1.reshape(-1, LANES)]
    )
    packed = packed + places.to_x(packed)
    hop = 1
    while hop < places.ctx:
        packed = packed + places.to_z(packed, hop)
        hop *= 2
    other = places.to_core(packed)
    cut = 3 * width // LANES
    sums = packed[:cut] + other[:cut]
    hop = 1
    while hop < tensor:
        sums = sums + lax.ppermute(sums, "tensor", [(t, t ^ hop) for t in range(tensor)])
        hop *= 2
    sums = sums.reshape(3, width // LANES, LANES)
    mine = pick(sums, (places.x * 2 + k) * places.ctx + places.z, 1)
    halves = places.ordered(k, packed[cut:], other[cut:])
    grad_bqkv = halves[:, : 3 * pairs].reshape(2, pairs, 3, LANES).transpose(2, 0, 1, 3).reshape(3, heads_width)
    grad_bfc1 = halves[:, 3 * pairs :].reshape(hidden_width)

    grad_w_qkv = grad_w_qkv.reshape(rows, 2, pairs, 3, LANES)
    grad_w_qkv = grad_w_qkv.transpose(0, 3, 1, 2, 4).reshape(rows, 3, heads_width)
    grad_w_out = grad_w_out.reshape(rows, heads_width).T
    return (
        output,
        grad_block,
        mine[:2],
        grad_w_qkv,
        grad_bqkv,
        grad_w_out,
        grad_fc1.reshape(rows, hidden_width),
        grad_bfc1,
        grad_fc2.reshape(rows, hidden_width).T,
        jnp.stack([mine[2], mine[2]]),
    )


def solution(mesh):
    split = ("x", "core", "ctx")
    in_specs = (
        P(("x", "core"), "ctx", None),
        P(None, split),
        P(split, None, "tensor"),
        P(None, "tensor"),
        P("tensor", split),
        P(split, "tensor"),
        P("tensor"),
        P("tensor", split),
        P(None, split),
        P(("x", "core"), "ctx", None),
    )
    out_specs = (
        P(("x", "core"), "ctx", None),
        P(("x", "core"), "ctx", None),
        P(None, split),
        P(split, None, "tensor"),
        P(None, "tensor"),
        P("tensor", split),
        P(split, "tensor"),
        P("tensor"),
        P("tensor", split),
        P(None, split),
    )

    axes = (2, 2, mesh.shape["ctx"], mesh.shape["tensor"])
    fine = Mesh(mesh.devices.reshape(axes), ("x", "core", "ctx", "tensor"))

    def whole(*arrays):
        places = Places(mesh, arrays[0].shape[0])
        inner = jax.shard_map(
            partial(shards, places), mesh=fine, in_specs=in_specs, out_specs=out_specs, check_vma=False
        )
        return inner(*arrays)

    return whole
```
